32 devices in a mesh: row: 4 (over y, x), col: 8 (over z, core).
Axes of the slice: x: 2, y: 2, z: 4, core: 2. Of those that a mesh axis runs over, the one named last changes fastest.
Arguments:
- pressure_guess: float32 [32, 512, 128], P('row', 'col'), may hold values from -3 to 3
- inv_density: float32 [32, 512, 128], P('row', 'col'), may hold values from 0.25 to 4
- source: float32 [32, 512, 128], P('row', 'col'), may hold values from -24 to 24
- plate_disp: float32 [16, 1024], P('row', 'col'), may hold values from -6 to 6
- plate_prev: float32 [16, 1024], P('row', 'col'), may hold values from -6 to 6
- thickness: float32 [16, 1024], P('row', 'col'), may hold values from 0.5 to 1.5
- face_owner: int32 [16384, 1], P(('row', 'col')), may hold values from 0 to 7; in each aligned block of 512 rows (0 to 511, 512 to 1023, ...) at most 128 rows name the same one
- face_elem: int32 [16384], P(('row', 'col')), may hold values from 0 to 511
- wet: int32 [16384], P(('row', 'col')), may hold values 0 or 1
Outputs:
- pressure: float32 [32, 512, 128], P('row', 'col')
- plate_next: float32 [16, 1024], P('row', 'col')
- face_motion: float32 [16384], P(('row', 'col'))
The draws below stay inside these ranges and needn't reach their ends.
Inputs may be any that keep to these rules, and one draw needn't show every extreme that they name: `face_owner`: among the 512 faces of one device no plating device is named by more than 128 faces, and some device names one plating device exactly 128 times.
All inputs are finite; a program needn't handle non-finite values. No bound on the sum of `wet` on one device may be relied on, other than what follows from the above.
Results may differ from the reference program's by a relative error of at most 0.00002.
Values sent between devices are 32-bit elements; how exact they have to be, the bound alone decides.
A program may use at most 64 MiB of HBM per device.

```python
import math
import jax
import jax.numpy as jnp
import numpy as np

FX = 8
FY = 64
FZ = 128
SWEEPS = 3
PXD = 4
PYD = 128
PSTEPS = 4
NX = 32
NY = 512
W = 512
FACES = 16384
CAP = 128
E_DEV = 512
PXT = 16
PYT = 1024
N_ROW = 4
N_COL = 8


def touch_ends(array, key, low, top_value):
    place = [jax.random.randint(jax.random.fold_in(key, axis), (), 0, length) for axis, length in enumerate(array.shape)]
    main_axis = array.shape.index(max(array.shape))
    next_to = place[:main_axis] + [(place[main_axis] + 1) % array.shape[main_axis]] + place[main_axis + 1:]
    return array.at[tuple(place)].set(low).at[tuple(next_to)].set(top_value)


def block_scale(key, shape, pieces, low, largest):
    factor_of = 1.0
    for dim, parts in pieces:
        steps = jax.random.uniform(jax.random.fold_in(jax.random.fold_in(key, 6), dim), (parts,), jnp.float32, low / len(pieces), largest / len(pieces))
        factor_of = factor_of * jnp.repeat(jnp.exp(steps), shape[dim] // parts).reshape((-1,) + (1,) * (len(shape) - 1 - dim))
    return factor_of


def deal_out(rng, own, number, rows, number_of, top, bound, skew):
    ranking = jax.random.permutation(rng, number_of)
    heavy_load, usual = shares(number_of, rows * top, bound, skew, True), shares(number_of, rows * top, bound, skew, False)
    places = jnp.arange(number_of)

    def named(tallies, offset_by):
        used = int((tallies > 0).sum())
        fixed = max(1, used // 4)
        moved = fixed + (places - fixed + offset_by * (used - fixed)) % max(1, number_of - fixed)
        return jnp.zeros((number_of,), jnp.int32).at[ranking[jnp.where(places < fixed, places, moved)]].set(jnp.asarray(tallies, jnp.int32))

    tallies = jnp.where(number % 4 == 0, named(heavy_load, number // 4), named(usual, number - number // 4 - 1))
    mixed = jax.random.permutation(jax.random.fold_in(own, 3), number_of)
    giver, receiver = mixed[0:number_of // 2 * 2:2], mixed[1:number_of // 2 * 2:2]
    margin = jnp.minimum(tallies[giver] - 1, bound - tallies[receiver]) // 2
    margin = jnp.where((giver == ranking[0]) | (receiver == ranking[0]) | (tallies[receiver] == 0), 0, jnp.maximum(margin, 0))
    moved = jax.random.randint(jax.random.fold_in(own, 4), (number_of // 2,), 0, 1 << 20) % (margin + 1)
    tallies = tallies.at[giver].add(-moved).at[receiver].add(moved)
    items = jnp.searchsorted(jnp.cumsum(tallies), jnp.arange(rows * top), side="right").astype(jnp.int32)
    table = items.reshape(top, rows).T
    table = table[jax.random.permutation(jax.random.fold_in(own, 1), rows)]
    offset_by = jax.random.randint(jax.random.fold_in(own, 2), (rows, 1), 0, top)
    return jnp.take_along_axis(table, (jnp.arange(top)[None, :] + offset_by) % top, axis=1)


def shares(count, total, bound, slope, full):
    weights = [(1 << 20) // math.isqrt(rank ** slope) + 1 for rank in range(1, count + 1)]
    largest = bound if full else min(bound, max(-(-total // count), total * weights[0] // sum(weights)))
    least = 1 if total - largest >= count - 1 else 0
    given, rest = [largest] + [least] * (count - 1), total - largest - least * (count - 1)
    while rest > 0:
        candidates = [i for i in range(1, count) if given[i] < largest] or [i for i in range(1, count) if given[i] < bound]
        pool, left = sum([weights[i] for i in candidates]), rest
        for i in candidates:
            more = min(bound - given[i], max(1, left * weights[i] // pool), rest)
            given[i] = given[i] + more
            rest = rest - more
    return np.array(given)


def normal_values(key, shape, width, bound, pieces=(), kind=jnp.bfloat16):
    loudness = block_scale(key, shape, pieces, -0.22, 0.18) if pieces else 1.0
    result = jax.random.normal(key, shape, jnp.float32) * width * loudness
    return jnp.minimum(jnp.maximum(result, -bound), bound).astype(kind)


def setup_inputs(seed: int = 0) -> dict:
    splits = jax.random.split(jax.random.key(seed), 10)
    pressure_guess = normal_values(splits[0], (NX, NY, FZ), 0.5, 3.0, ((0, 4), (1, 8)), jnp.float32)
    inv_density = jnp.clip(jnp.exp(math.log(4.0) - 2.7725887 * jax.random.uniform(splits[1], (NX, NY, FZ), jnp.float32) ** block_scale(splits[1], (NX, NY, FZ), ((0, 4), (1, 8)), -0.2, 0.2)), 0.25, 4.0)
    source = normal_values(splits[2], (NX, NY, FZ), 4.0, 24.0, ((0, 4), (1, 8)), jnp.float32)
    plate_disp = normal_values(splits[3], (PXT, PYT), 1.0, 6.0, ((0, 4), (1, 8)), jnp.float32)
    plate_prev = normal_values(splits[4], (PXT, PYT), 1.0, 6.0, ((0, 4), (1, 8)), jnp.float32)
    thickness = jnp.clip(jnp.exp(math.log(1.5) - 1.0986123 * jax.random.uniform(splits[5], (PXT, PYT), jnp.float32) ** block_scale(splits[5], (PXT, PYT), ((0, 4), (1, 8)), -0.2, 0.2)), 0.5, 1.5)
    face_owner_keys = jax.random.split(jax.random.fold_in(splits[6], 1), FACES // W)
    face_owner_turns = jax.random.permutation(jax.random.fold_in(splits[6], 3), FACES // W)
    face_owner = jax.vmap(lambda own, number: deal_out(jax.random.fold_in(splits[6], 2), own, number, W, N_COL, 1, CAP, 1))(face_owner_keys, face_owner_turns).reshape((FACES, 1))
    face_elem = touch_ends(jax.random.randint(splits[7], (FACES,), 0, E_DEV), jax.random.fold_in(splits[7], 1), 0, E_DEV - 1).astype(jnp.int32)
    wet = touch_ends((jax.random.randint(splits[8], (FACES,), 0, 4) < 3).astype(jnp.int32), jax.random.fold_in(splits[8], 1), 0, 1)
    return dict(pressure_guess=pressure_guess, inv_density=inv_density, source=source, plate_disp=plate_disp, plate_prev=plate_prev, thickness=thickness, face_owner=face_owner, face_elem=face_elem, wet=wet)


OMEGA = 0.8
BEND = 0.006
LOADC = 0.25


def relax(field_ext, coeff_ext, source, inside):
    padded_field = jnp.pad(field_ext, ((0, 0), (0, 0), (1, 1)))
    padded_coeff = jnp.pad(coeff_ext, ((0, 0), (0, 0), (1, 1)))
    center = padded_field[1:-1, 1:-1, 1:-1]
    center_coeff = padded_coeff[1:-1, 1:-1, 1:-1]
    windows = ((slice(2, None), slice(1, -1), slice(1, -1)),
               (slice(0, -2), slice(1, -1), slice(1, -1)),
               (slice(1, -1), slice(2, None), slice(1, -1)),
               (slice(1, -1), slice(0, -2), slice(1, -1)),
               (slice(1, -1), slice(1, -1), slice(2, None)),
               (slice(1, -1), slice(1, -1), slice(0, -2)))
    diagonal = jnp.zeros_like(center)
    inflow = jnp.zeros_like(center)
    for window in windows:
        beta = 0.5 * (center_coeff + padded_coeff[window])
        diagonal = diagonal + beta
        inflow = inflow + beta * padded_field[window]
    if inside is not None:
        diagonal = diagonal + (1.0 - inside)
    updated = center + OMEGA * (source - (diagonal * center - inflow)) / diagonal
    if inside is not None:
        updated = updated * inside
    return updated


def laplace(field_ext):
    return (field_ext[2:, 1:-1] + field_ext[:-2, 1:-1] + field_ext[1:-1, 2:]
            + field_ext[1:-1, :-2] - 4.0 * field_ext[1:-1, 1:-1])


def bilaplace(field_ext, thick_ext):
    curvature = laplace(field_ext)
    moment = BEND * thick_ext[1:-1, 1:-1] ** 3 * curvature
    return laplace(moment)


def reference(pressure_guess, inv_density, source, plate_disp, plate_prev, thickness, face_owner, face_elem, wet):
    pressure = pressure_guess
    coeff_ext = jnp.pad(inv_density, ((1, 1), (1, 1), (0, 0)))
    for sweep_index in range(SWEEPS):
        pressure = relax(jnp.pad(pressure, ((1, 1), (1, 1), (0, 0))), coeff_ext, source, None)
    face_press = pressure[:, :, 0].reshape(N_ROW, FX, N_COL, FY).transpose(0, 2, 1, 3).reshape(-1)
    values = face_press * wet.astype(face_press.dtype)
    face_row = jnp.arange(FACES, dtype=jnp.int32) // (N_COL * FX * FY)
    owner = face_owner[:, 0]
    plate_i = face_row * PXD + face_elem // PYD
    plate_j = owner * PYD + face_elem % PYD
    flat_index = (plate_i * (PYD * N_COL) + plate_j).astype(jnp.int32)
    loads = jax.ops.segment_sum(values, flat_index, num_segments=PXD * N_ROW * PYD * N_COL)
    loads = loads.reshape(PXD * N_ROW, PYD * N_COL)
    current = plate_disp
    previous = plate_prev
    thick_ext = jnp.pad(thickness, 2)
    for step_index in range(PSTEPS):
        bending = bilaplace(jnp.pad(current, 2), thick_ext)
        upcoming = 2.0 * current - previous + (LOADC * loads - bending) / thickness
        previous = current
        current = upcoming
    face_motion = current.reshape(-1)[flat_index]
    return pressure, current, face_motion
```

```python
import functools

import jax
import jax.numpy as jnp
from jax import lax
from jax.experimental import pallas as pl
from jax.experimental.pallas import tpu as pltpu
from jax.sharding import PartitionSpec as P

SWEEPS = 3
PSTEPS = 4
OMEGA = 0.8
BEND = 0.006
LOADC = 0.25

LANES = 128
NEAR = 2
WIN = 2 * NEAR + 1
MESH = pl.DeviceIdType.MESH
NT = (((1,), (1,)), ((), ()))
F32 = jnp.float32
BF16 = jnp.bfloat16


def times(count, body):
    if count <= 32:
        for step in range(count):
            body(step)
    else:
        lax.fori_loop(0, count, lambda step, carry: (body(step), carry)[1], 0)


def three(value):
    a = value.astype(BF16)
    rest = value - a.astype(F32)
    b = rest.astype(BF16)
    c = (rest - b.astype(F32)).astype(BF16)
    return a, b, c


def kernel(
    rows, cols,
    p_ref, c_ref, s_ref, disp_ref, prev_ref, thick_ref, owner_ref, elem_ref, wet_ref,
    out_ref, plate_ref, motion_ref,
    pa, pb, wt, xrecv, ysend, yrecv,
    ibuf, vbuf, ubuf, sbuf, srecv, lslab, lrecv, win, lwin, onehot, spread, own_hot, uslab,
    fsend, frecv, gsend, grecv, tsend, trecv, rsend, rrecv,
):
    nx, ny, nz = p_ref.shape
    px, py = disp_ref.shape
    frows = owner_ref.shape[0]
    high = cols * px
    r, c = lax.axis_index("row"), lax.axis_index("col")
    last = nx - 1

    def row_ok(d):
        return jnp.logical_and(r + d >= 0, r + d < rows)

    shifts = [d for d in range(-NEAR, NEAR + 1) if d != 0]

    barrier = pltpu.get_barrier_semaphore()
    peers = cols - 1
    for d in shifts:
        @pl.when(row_ok(d))
        def _(d=d):
            pl.semaphore_signal(barrier, inc=1, device_id=(r + d, c), device_id_type=MESH)
        peers = peers + row_ok(d).astype(jnp.int32)

    def greet(step):
        pl.semaphore_signal(barrier, inc=1, device_id=(r, lax.rem(c + 1 + step, cols)), device_id_type=MESH)

    times(cols - 1, greet)

    gives = [r < rows - 1, r > 0, c < cols - 1, c > 0]
    takes = [r > 0, r < rows - 1, c > 0, c < cols - 1]
    fields = [c_ref, p_ref, pa, pb]

    def halo(phase, way):
        if way < 2:
            src = fields[phase].at[last if way == 0 else 0]
            dst = xrecv.at[phase, way]
            to = (r + 1 - 2 * way, c)
        else:
            src = ysend.at[phase, way - 2]
            dst = yrecv.at[phase, way - 2]
            to = (r, c + 1 - 2 * (way - 2))
        return pltpu.make_async_remote_copy(
            src_ref=src, dst_ref=dst, send_sem=fsend.at[phase, way], recv_sem=frecv.at[phase, way],
            device_id=to, device_id_type=MESH,
        )

    def halo_start(phase, ways):
        for way in ways:
            @pl.when(gives[way])
            def _(way=way):
                halo(phase, way).start()

    def halo_wait(phase, ways):
        for way in ways:
            @pl.when(takes[way])
            def _(way=way):
                halo(phase, way).wait_recv()

    def halo_sent(phase):
        for way in range(4):
            @pl.when(gives[way])
            def _(way=way):
                halo(phase, way).wait_send()

    def pack(phase):
        field = fields[phase]
        for x in range(nx):
            ysend[phase, 0, x:x + 1, :] = field[x, ny - 1:ny, :]
            ysend[phase, 1, x:x + 1, :] = field[x, 0:1, :]

    def gather(which, buf, step):
        return pltpu.make_async_remote_copy(
            src_ref=buf.at[c], dst_ref=buf.at[c], send_sem=gsend.at[which, step], recv_sem=grecv.at[which, step],
            device_id=(r, lax.rem(c + 1 + step, cols)), device_id_type=MESH,
        )

    def gather_start(which, buf):
        times(cols - 1, lambda step: gather(which, buf, step).start())

    def gather_wait(which, buf):
        def one(step):
            frm = lax.rem(c + cols - 1 - step, cols)
            pltpu.make_async_remote_copy(
                src_ref=buf.at[frm], dst_ref=buf.at[frm], send_sem=gsend.at[which, step],
                recv_sem=grecv.at[which, step], device_id=(r, frm), device_id_type=MESH,
            ).wait_recv()
        times(cols - 1, one)

    def gather_sent(which, buf):
        times(cols - 1, lambda step: gather(which, buf, step).wait_send())

    def beside(way):
        return pltpu.make_async_remote_copy(
            src_ref=sbuf.at[1], dst_ref=sbuf.at[2 * way], send_sem=tsend.at[way], recv_sem=trecv.at[way],
            device_id=(r, c + 1 - 2 * way), device_id_type=MESH,
        )

    def along(which, d):
        src = sbuf if which == 0 else lslab.at[pl.ds(c, 3)]
        dst = (srecv if which == 0 else lrecv).at[NEAR - d]
        return pltpu.make_async_remote_copy(
            src_ref=src, dst_ref=dst, send_sem=rsend.at[which, NEAR - d], recv_sem=rrecv.at[which, NEAR - d],
            device_id=(r + d, c), device_id_type=MESH,
        )

    def along_each(which, act, back=False):
        for d in shifts:
            @pl.when(row_ok(-d if back else d))
            def _(d=d):
                act(along(which, d))

    pack(0)
    pack(1)
    ibuf[c] = owner_ref[...] * (px * py) + elem_ref[...]
    sbuf[1, 0] = disp_ref[...]
    sbuf[1, 1] = prev_ref[...]
    sbuf[1, 2] = thick_ref[...]
    for way in range(4):
        @pl.when(jnp.logical_not(takes[way]))
        def _(way=way):
            if way < 2:
                for phase in range(4):
                    xrecv[phase, way] = jnp.zeros((ny, nz), F32)
            else:
                for phase in range(4):
                    yrecv[phase, way - 2] = jnp.zeros((nx, nz), F32)
                sbuf[2 * (way - 2)] = jnp.zeros((3, px, py), F32)
    for d in shifts:
        @pl.when(jnp.logical_not(row_ok(d)))
        def _(d=d):
            srecv[NEAR + d] = jnp.zeros(srecv.shape[1:], F32)
            lrecv[NEAR + d] = jnp.zeros(lrecv.shape[1:], F32)
    lslab[0] = jnp.zeros((px, py), F32)
    lslab[cols + 1] = jnp.zeros((px, py), F32)

    pl.semaphore_wait(barrier, peers)

    halo_start(0, (0, 1))
    halo_start(1, (0, 1))
    halo_start(0, (2, 3))
    halo_start(1, (2, 3))
    for way in range(2):
        @pl.when(gives[2 + way])
        def _(way=way):
            beside(way).start()
    gather_start(0, ibuf)

    row_id = lax.broadcasted_iota(jnp.int32, (ny, nz), 0)
    lane_id = lax.broadcasted_iota(jnp.int32, (ny, nz), 1)

    def around(plane, phase, x):
        low = jnp.where(row_id == 0, yrecv[phase, 0, x:x + 1, :], pltpu.roll(plane, 1, 0))
        up = jnp.where(row_id == ny - 1, yrecv[phase, 1, x:x + 1, :], pltpu.roll(plane, ny - 1, 0))
        left = jnp.where(lane_id == 0, 0.0, pltpu.roll(plane, 1, 1))
        right = jnp.where(lane_id == nz - 1, 0.0, pltpu.roll(plane, nz - 1, 1))
        return low, up, left, right

    def beneath(field, phase, x):
        return (
            field[x - 1] if x > 0 else xrecv[phase, 0],
            field[x + 1] if x < last else xrecv[phase, 1],
        )

    def coefficients(x):
        mid = c_ref[x]
        six = beneath(c_ref, 0, x) + around(mid, 0, x)
        diag = 3.0 * mid + 0.5 * (((six[0] + six[1]) + (six[2] + six[3])) + (six[4] + six[5]))
        scale = OMEGA / diag
        half = 0.5 * scale
        wt[0, x] = scale * s_ref[x]
        for i in range(6):
            wt[1 + i, x] = half * (mid + six[i])

    def sweep(src, dst, phase, x):
        mid = src[x]
        six = beneath(src, phase, x) + around(mid, phase, x)
        total = (1.0 - OMEGA) * mid + wt[0, x]
        for i in range(6):
            total = total + wt[1 + i, x] * six[i]
        dst[x] = total

    halo_wait(0, (2, 3))
    for x in range(1, last):
        coefficients(x)
    halo_wait(1, (2, 3))
    for x in range(1, last):
        sweep(p_ref, pa, 1, x)
    halo_wait(0, (0, 1))
    for x in (0, last):
        coefficients(x)
    halo_wait(1, (0, 1))
    for x in (0, last):
        sweep(p_ref, pa, 1, x)
    halo_start(2, (0, 1))
    pack(2)
    halo_start(2, (2, 3))

    for way in range(2):
        @pl.when(takes[2 + way])
        def _(way=way):
            beside(way).wait_recv()
    along_each(0, lambda copy: copy.start())

    halo_wait(2, (2, 3))
    for x in range(1, last):
        sweep(pa, pb, 2, x)
    halo_wait(2, (0, 1))
    for x in (0, last):
        sweep(pa, pb, 2, x)
    halo_start(3, (0, 1))
    pack(3)
    halo_start(3, (2, 3))

    gather_wait(0, ibuf)
    lo_id = lax.broadcasted_iota(jnp.int32, (py, LANES), 0)
    hi_id = lax.broadcasted_iota(jnp.int32, (high, LANES), 0)

    def mark(dev, j):
        place = lax.rem(ibuf[dev, j:j + 1, :], py)
        return jnp.where(lo_id == place, 1.0, 0.0).astype(BF16)

    def hot(dev):
        for j in range(frows):
            onehot[dev, :, j * LANES:(j + 1) * LANES] = mark(dev, j)

    times(cols, hot)
    for j in range(frows):
        own_hot[:, j * LANES:(j + 1) * LANES] = mark(c, j)

    along_each(0, lambda copy: copy.wait_recv(), back=True)
    tall = win.shape[1]
    win[:, WIN * px:, :] = jnp.zeros((3, tall - WIN * px, 3 * py), F32)
    for w in range(WIN):
        for k in range(3):
            for f in range(3):
                block = sbuf[k, f] if w == NEAR else srecv[w, k, f]
                win[f, w * px:(w + 1) * px, k * py:(k + 1) * py] = block
    current, previous, thick = win[0], win[1], win[2]
    inside = thick > 0.0
    inverse = jnp.where(inside, 1.0 / jnp.where(inside, thick, 1.0), 0.0)
    stiff = BEND * (thick * thick * thick)

    def laplace(u):
        return (
            pltpu.roll(u, 1, 0) + pltpu.roll(u, tall - 1, 0)
            + pltpu.roll(u, 1, 1) + pltpu.roll(u, 3 * py - 1, 1) - 4.0 * u
        )

    def free(now, before):
        return 2.0 * now - before - laplace(stiff * laplace(now)) * inverse

    ahead = free(current, previous)

    halo_wait(3, (2, 3))
    for x in range(1, last):
        sweep(pb, out_ref, 3, x)
    halo_wait(3, (0, 1))
    for x in (0, last):
        sweep(pb, out_ref, 3, x)

    first = (lax.broadcasted_iota(jnp.int32, (8, nz), 1) == 0).astype(F32)
    field = out_ref[...].reshape(nx * ny, nz)
    face = lax.dot_general(first, field, NT, precision=lax.Precision.HIGHEST, preferred_element_type=F32)
    for j in range(frows):
        vbuf[c, j:j + 1, :] = face[0:1, j * LANES:(j + 1) * LANES] * wet_ref[j:j + 1, :].astype(F32)
    gather_start(1, vbuf)
    gather_wait(1, vbuf)

    chunk = spread.shape[0]
    loads = jnp.zeros((3 * high, py), F32)
    for base in range(0, cols, chunk):
        def fill(dev):
            for j in range(frows):
                level = lax.div(ibuf[base + dev, j:j + 1, :], py)
                keep = hi_id == level
                for part, v in enumerate(three(vbuf[base + dev, j:j + 1, :])):
                    tile = jnp.where(keep, v.astype(F32), 0.0).astype(BF16)
                    spread[dev, part * high:(part + 1) * high, j * LANES:(j + 1) * LANES] = tile

        times(chunk, fill)
        for dev in range(chunk):
            loads = loads + lax.dot_general(
                spread[dev], onehot[base + dev], NT, preferred_element_type=F32
            )
    slab = loads[:high] + loads[high:2 * high] + loads[2 * high:]
    for dev in range(cols):
        lslab[1 + dev] = slab[dev * px:(dev + 1) * px]
    along_each(1, lambda copy: copy.start())
    along_each(1, lambda copy: copy.wait_recv(), back=True)
    lwin[WIN * px:, :] = jnp.zeros((tall - WIN * px, 3 * py), F32)
    for w in range(WIN):
        for k in range(3):
            block = lslab[c + k] if w == NEAR else lrecv[w, k]
            lwin[w * px:(w + 1) * px, k * py:(k + 1) * py] = block
    push = LOADC * lwin[...] * inverse

    previous, current = current, ahead + push
    for _ in range(PSTEPS - 1):
        previous, current = current, free(current, previous) + push
    mine = current[NEAR * px:(NEAR + 1) * px, py:2 * py]
    plate_ref[...] = mine
    ubuf[c] = mine
    gather_start(2, ubuf)
    gather_wait(2, ubuf)

    for dev in range(cols):
        uslab[dev * px:(dev + 1) * px, :] = ubuf[dev]
    parts = three(uslab[...])
    picked = lax.dot_general(
        jnp.concatenate(parts, axis=0), own_hot[...], (((1,), (0,)), ((), ())), preferred_element_type=F32
    )
    picked = picked[:high] + picked[high:2 * high] + picked[2 * high:]
    for j in range(frows):
        level = lax.div(ibuf[c, j:j + 1, :], py)
        part = jnp.where(hi_id == level, picked[:, j * LANES:(j + 1) * LANES], 0.0)
        motion_ref[j:j + 1, :] = jnp.sum(part, axis=0, keepdims=True)

    for phase in range(4):
        halo_sent(phase)
    for way in range(2):
        @pl.when(gives[2 + way])
        def _(way=way):
            beside(way).wait_send()
    for which, buf in enumerate((ibuf, vbuf, ubuf)):
        gather_sent(which, buf)
    for which in range(2):
        along_each(which, lambda copy: copy.wait_send())


def shards(rows, cols, pressure, density, source, disp, prev, thick, owner, elem, wet):
    nx, ny, nz = pressure.shape
    px, py = disp.shape
    faces = elem.shape[0]
    frows = faces // LANES
    high = cols * px
    tall = -(-WIN * px // 8) * 8
    chunk = 8 if cols % 8 == 0 else 1
    vmem = pl.BlockSpec(memory_space=pltpu.VMEM)
    dma = pltpu.SemaphoreType.DMA
    pressure, plate, motion = pl.pallas_call(
        functools.partial(kernel, rows, cols),
        out_shape=(
            jax.ShapeDtypeStruct(pressure.shape, F32),
            jax.ShapeDtypeStruct(disp.shape, F32),
            jax.ShapeDtypeStruct((frows, LANES), F32),
        ),
        in_specs=[vmem] * 9,
        out_specs=(vmem,) * 3,
        scratch_shapes=[
            pltpu.VMEM((nx, ny, nz), F32),
            pltpu.VMEM((nx, ny, nz), F32),
            pltpu.VMEM((7, nx, ny, nz), F32),
            pltpu.VMEM((4, 2, ny, nz), F32),
            pltpu.VMEM((4, 2, nx, nz), F32),
            pltpu.VMEM((4, 2, nx, nz), F32),
            pltpu.VMEM((cols, frows, LANES), jnp.int32),
            pltpu.VMEM((cols, frows, LANES), F32),
            pltpu.VMEM((cols, px, py), F32),
            pltpu.VMEM((3, 3, px, py), F32),
            pltpu.VMEM((WIN, 3, 3, px, py), F32),
            pltpu.VMEM((cols + 2, px, py), F32),
            pltpu.VMEM((WIN, 3, px, py), F32),
            pltpu.VMEM((3, tall, 3 * py), F32),
            pltpu.VMEM((tall, 3 * py), F32),
            pltpu.VMEM((cols, py, faces), BF16),
            pltpu.VMEM((chunk, 3 * high, faces), BF16),
            pltpu.VMEM((py, faces), BF16),
            pltpu.VMEM((high, py), F32),
            dma((4, 4)), dma((4, 4)),
            dma((3, cols - 1)), dma((3, cols - 1)),
            dma((2,)), dma((2,)),
            dma((2, WIN)), dma((2, WIN)),
        ],
        compiler_params=pltpu.CompilerParams(
            collective_id=0, has_side_effects=True, vmem_limit_bytes=48 * 1024 * 1024
        ),
        name="slamming",
    )(
        pressure, density, source, disp, prev, thick,
        owner.reshape(frows, LANES), elem.reshape(frows, LANES), wet.reshape(frows, LANES),
    )
    return pressure, plate, motion.reshape(faces)


def solution(mesh):
    rows, cols = mesh.shape["row"], mesh.shape["col"]
    placed = (
        P("row", "col", None),
        P("row", "col", None),
        P("row", "col", None),
        P("row", "col"),
        P("row", "col"),
        P("row", "col"),
        P(("row", "col"), None),
        P(("row", "col")),
        P(("row", "col")),
    )
    return jax.shard_map(
        functools.partial(shards, rows, cols),
        mesh=mesh,
        in_specs=placed,
        out_specs=(P("row", "col", None), P("row", "col"), P(("row", "col"))),
        check_vma=False,
    )
```

```python
import functools

import jax
import jax.numpy as jnp
from jax import lax
from jax.experimental import pallas as pl
from jax.experimental.pallas import tpu as pltpu
from jax.sharding import PartitionSpec as P

SWEEPS = 3
PSTEPS = 4
OMEGA = 0.8
BEND = 0.006
LOADC = 0.25

LANES = 128
NEAR = 2
WIN = 2 * NEAR + 1
MESH = pl.DeviceIdType.MESH
NT = (((1,), (1,)), ((), ()))
F32 = jnp.float32
BF16 = jnp.bfloat16


def times(count, body):
    if count <= 32:
        for step in range(count):
            body(step)
    else:
        lax.fori_loop(0, count, lambda step, carry: (body(step), carry)[1], 0)


def three(value):
    a = value.astype(BF16)
    rest = value - a.astype(F32)
    b = rest.astype(BF16)
    c = (rest - b.astype(F32)).astype(BF16)
    return a, b, c


def kernel(
    rows, cols,
    p_hbm, c_hbm, s_hbm, disp_hbm, prev_hbm, thick_hbm, owner_hbm, elem_hbm, wet_hbm,
    out_ref, plate_ref, motion_ref,
    p_ref, c_ref, s_ref, small, faces_in,
    pa, pb, wt, xrecv, ysend, yrecv,
    thin, gbuf, vbuf, ubuf, srecv, lslab, lrecv, win, lwin, onehot, spread, own_hot, uslab,
    lsem, fsend, frecv, gsend, grecv, tsend, trecv, rsend, rrecv,
):
    nx, ny, nz = p_ref.shape
    px, py = small.shape[1:]
    frows = faces_in.shape[1]
    high = cols * px
    last = nx - 1
    reach = SWEEPS
    r, c = lax.axis_index("row"), lax.axis_index("col")

    def row_ok(d):
        return jnp.logical_and(r + d >= 0, r + d < rows)

    def both_ok(dr, dc):
        return jnp.logical_and(row_ok(dr), jnp.logical_and(c + dc >= 0, c + dc < cols))

    shifts = [d for d in range(-NEAR, NEAR + 1) if d != 0]
    corners = [(dr, dc) for dr in (-1, 1) for dc in (-1, 1)]
    blocks = [(-1, 0), (1, 0), (0, -1), (0, 1)] + corners

    loads_in = [
        (c_hbm, c_ref), (p_hbm, p_ref), (s_hbm, s_ref),
        (disp_hbm, small.at[0]), (prev_hbm, small.at[1]), (thick_hbm, small.at[2]),
        (owner_hbm, faces_in.at[0]), (elem_hbm, faces_in.at[1]), (wet_hbm, faces_in.at[2]),
    ]
    loads_in = [pltpu.make_async_copy(a, b, lsem.at[i]) for i, (a, b) in enumerate(loads_in)]
    for copy in loads_in:
        copy.start()

    barrier = pltpu.get_barrier_semaphore()
    peers = cols - 1
    for dr, dc in [(d, 0) for d in shifts] + corners:
        @pl.when(both_ok(dr, dc))
        def _(dr=dr, dc=dc):
            pl.semaphore_signal(barrier, inc=1, device_id=(r + dr, c + dc), device_id_type=MESH)
        peers = peers + both_ok(dr, dc).astype(jnp.int32)

    def greet(step):
        pl.semaphore_signal(barrier, inc=1, device_id=(r, lax.rem(c + 1 + step, cols)), device_id_type=MESH)

    times(cols - 1, greet)

    gives = [r < rows - 1, r > 0, c < cols - 1, c > 0]
    takes = [r > 0, r < rows - 1, c > 0, c < cols - 1]
    fields = [c_ref, p_ref, pa, pb]

    def halo(phase, way):
        if way < 2:
            src = fields[phase].at[last if way == 0 else 0]
            dst = xrecv.at[phase, way]
            to = (r + 1 - 2 * way, c)
        else:
            src = ysend.at[phase, way - 2]
            dst = yrecv.at[phase, way - 2]
            to = (r, c + 1 - 2 * (way - 2))
        return pltpu.make_async_remote_copy(
            src_ref=src, dst_ref=dst, send_sem=fsend.at[phase, way], recv_sem=frecv.at[phase, way],
            device_id=to, device_id_type=MESH,
        )

    def halo_start(phase, ways):
        for way in ways:
            @pl.when(gives[way])
            def _(way=way):
                halo(phase, way).start()

    def halo_wait(phase, ways):
        for way in ways:
            @pl.when(takes[way])
            def _(way=way):
                halo(phase, way).wait_recv()

    def halo_sent(phase):
        for way in range(4):
            @pl.when(gives[way])
            def _(way=way):
                halo(phase, way).wait_send()

    def pack(phase):
        field = fields[phase]
        for x in range(nx):
            ysend[phase, 0, x:x + 1, :] = field[x, ny - 1:ny, :]
            ysend[phase, 1, x:x + 1, :] = field[x, 0:1, :]

    def slot(which, dev):
        return gbuf.at[:, dev] if which == 0 else vbuf.at[dev]

    def gather(which, step):
        return pltpu.make_async_remote_copy(
            src_ref=slot(which, c), dst_ref=slot(which, c), send_sem=gsend.at[which, step],
            recv_sem=grecv.at[which, step], device_id=(r, lax.rem(c + 1 + step, cols)), device_id_type=MESH,
        )

    def gather_start(which):
        times(cols - 1, lambda step: gather(which, step).start())

    def gather_wait(which):
        def one(step):
            frm = lax.rem(c + cols - 1 - step, cols)
            pltpu.make_async_remote_copy(
                src_ref=slot(which, frm), dst_ref=slot(which, frm), send_sem=gsend.at[which, step],
                recv_sem=grecv.at[which, step], device_id=(r, frm), device_id_type=MESH,
            ).wait_recv()
        times(cols - 1, one)

    def gather_sent(which):
        times(cols - 1, lambda step: gather(which, step).wait_send())

    def along(which, d):
        src = gbuf.at[pl.ds(1, 3)] if which == 0 else lslab
        dst = (srecv if which == 0 else lrecv).at[NEAR - d]
        return pltpu.make_async_remote_copy(
            src_ref=src, dst_ref=dst, send_sem=rsend.at[which, NEAR - d], recv_sem=rrecv.at[which, NEAR - d],
            device_id=(r + d, c), device_id_type=MESH,
        )

    def along_each(which, act, back=False):
        for d in shifts:
            @pl.when(row_ok(-d if back else d))
            def _(d=d):
                act(along(which, d))

    far = {-1: (0, reach), 0: (reach, nx), 1: (reach + nx, reach)}

    def skin(dr, dc):
        first = {-1: reach, 0: reach, 1: nx}[dr]
        at, count = far[-dr]
        return pltpu.make_async_remote_copy(
            src_ref=thin.at[1, pl.ds(first, count)], dst_ref=thin.at[1 - dc, pl.ds(at, count)],
            send_sem=tsend.at[3 * dr + dc + 4], recv_sem=trecv.at[3 * dr + dc + 4],
            device_id=(r + dr, c + dc), device_id_type=MESH,
        )

    for way in range(4):
        @pl.when(jnp.logical_not(takes[way]))
        def _(way=way):
            if way < 2:
                for phase in range(4):
                    xrecv[phase, way] = jnp.zeros((ny, nz), F32)
            else:
                for phase in range(4):
                    yrecv[phase, way - 2] = jnp.zeros((nx, nz), F32)
    for dr, dc in blocks:
        @pl.when(jnp.logical_not(both_ok(dr, dc)))
        def _(dr=dr, dc=dc):
            at, count = far[dr]
            thin[1 + dc, at:at + count] = jnp.zeros((count, 8, LANES), F32)
    for d in shifts:
        @pl.when(jnp.logical_not(row_ok(d)))
        def _(d=d):
            srecv[NEAR + d] = jnp.zeros(srecv.shape[1:], F32)
            lrecv[NEAR + d] = jnp.zeros(lrecv.shape[1:], F32)

    loads_in[0].wait()
    pack(0)
    loads_in[1].wait()
    pack(1)
    loads_in[2].wait()
    depth = lax.broadcasted_iota(jnp.int32, (8, nz), 0)
    layer = lax.broadcasted_iota(jnp.int32, (8, nz), 1)
    top = jnp.logical_and(depth == layer, depth < 4).astype(F32)
    low = (depth == layer + 4).astype(F32)

    def take(which, field):
        return lax.dot_general(
            which, field[...].reshape(nx * ny, nz), NT, precision=lax.Precision.HIGHEST,
            preferred_element_type=F32,
        )

    hull = take(top, p_ref) + take(low, c_ref)
    feed = take(top, s_ref)
    near = lax.broadcasted_iota(jnp.int32, (8, LANES), 1)
    for x in range(nx):
        v = (x // 2) * LANES
        one, two = hull[:, v:v + LANES], feed[:, v:v + LANES]
        if x % 2 == 0:
            two = pltpu.roll(two, ny, 1)
        else:
            one = pltpu.roll(one, ny, 1)
        thin[1, reach + x] = jnp.where(near < ny, one, two)
    for copy in loads_in[3:]:
        copy.wait()
    gbuf[0, c] = (faces_in[0] * (px * py) + faces_in[1]).astype(F32)
    for f in range(3):
        gbuf[1 + f, c] = small[f]

    pl.semaphore_wait(barrier, peers)

    for dr, dc in blocks:
        @pl.when(both_ok(dr, dc))
        def _(dr=dr, dc=dc):
            skin(dr, dc).start()
    halo_start(0, (0, 1))
    halo_start(1, (0, 1))
    halo_start(0, (2, 3))
    halo_start(1, (2, 3))
    gather_start(0)

    row_id = lax.broadcasted_iota(jnp.int32, (ny, nz), 0)
    lane_id = lax.broadcasted_iota(jnp.int32, (ny, nz), 1)

    def around(plane, phase, x):
        low = jnp.where(row_id == 0, yrecv[phase, 0, x:x + 1, :], pltpu.roll(plane, 1, 0))
        up = jnp.where(row_id == ny - 1, yrecv[phase, 1, x:x + 1, :], pltpu.roll(plane, ny - 1, 0))
        left = jnp.where(lane_id == 0, 0.0, pltpu.roll(plane, 1, 1))
        right = jnp.where(lane_id == nz - 1, 0.0, pltpu.roll(plane, nz - 1, 1))
        return low, up, left, right

    def beneath(field, phase, x):
        return (
            field[x - 1] if x > 0 else xrecv[phase, 0],
            field[x + 1] if x < last else xrecv[phase, 1],
        )

    def weights(mid, six):
        diag = 3.0 * mid + 0.5 * (((six[0] + six[1]) + (six[2] + six[3])) + (six[4] + six[5]))
        scale = OMEGA / diag
        half = 0.5 * scale
        return scale, [half * (mid + one) for one in six]

    def coefficients(x):
        mid = c_ref[x]
        scale, six = weights(mid, beneath(c_ref, 0, x) + around(mid, 0, x))
        wt[0, x] = scale * s_ref[x]
        for i in range(6):
            wt[1 + i, x] = six[i]

    def sweep(src, dst, phase, x):
        mid = src[x]
        six = beneath(src, phase, x) + around(mid, phase, x)
        total = (1.0 - OMEGA) * mid + wt[0, x]
        for i in range(6):
            total = total + wt[1 + i, x] * six[i]
        dst[x] = total

    halo_wait(0, (2, 3))
    for x in range(1, last):
        coefficients(x)
    halo_wait(1, (2, 3))
    for x in range(1, last):
        sweep(p_ref, pa, 1, x)

    for dr, dc in blocks:
        @pl.when(both_ok(-dr, -dc))
        def _(dr=dr, dc=dc):
            skin(dr, dc).wait_recv()
    half = ny // 2
    ps, cs, ss = [], [], []
    for x in range(nx + 2 * reach):
        left, own, right = thin[0, x], thin[1, x], thin[2, x]
        side = jnp.where(near >= half, left, right)
        middle = jnp.logical_and(near >= half, near < half + ny)
        pc = jnp.where(middle, pltpu.roll(own, half, 1), pltpu.roll(side, half + ny, 1))
        side = jnp.where(near >= ny + half, left, right)
        ss.append(jnp.where(middle, pltpu.roll(own, half + ny, 1), pltpu.roll(side, half, 1)))
        ps.append(jnp.where(depth[:, :LANES] < 4, pc, 0.0))
        cs.append(jnp.where(depth[:, :LANES] < 4, pltpu.roll(pc, 4, 0), 0.0))

    def thin_six(field, x):
        mid = field[x]
        return (
            field[x - 1], field[x + 1], pltpu.roll(mid, 1, 1), pltpu.roll(mid, LANES - 1, 1),
            jnp.where(depth == 0, 0.0, pltpu.roll(mid, 1, 0)), pltpu.roll(mid, 7, 0),
        )

    shares = {}
    for x in range(1, nx + 2 * reach - 1):
        scale, six = weights(cs[x], thin_six(cs, x))
        shares[x] = (scale * ss[x], six, cs[x] > 0.0)
    for level in range(1, reach + 1):
        new = list(ps)
        for x in range(level, nx + 2 * reach - level):
            fixed, six, inside = shares[x]
            total = (1.0 - OMEGA) * ps[x] + fixed
            for a, b in zip(six, thin_six(ps, x)):
                total = total + a * b
            new[x] = jnp.where(inside, total, 0.0)
        ps = new
    for j in range(frows):
        even = pltpu.roll(ps[reach + 2 * j], LANES - half, 1)
        odd = pltpu.roll(ps[reach + 2 * j + 1], half, 1)
        face = jnp.where(near < ny, even, odd)[0:1]
        vbuf[c, j:j + 1, :] = face * faces_in[2, j:j + 1, :].astype(F32)
    gather_start(1)

    halo_wait(0, (0, 1))
    for x in (0, last):
        coefficients(x)
    halo_wait(1, (0, 1))
    for x in (0, last):
        sweep(p_ref, pa, 1, x)
    halo_start(2, (0, 1))
    pack(2)
    halo_start(2, (2, 3))

    gather_wait(0)
    along_each(0, lambda copy: copy.start())
    lo_id = lax.broadcasted_iota(jnp.int32, (py, LANES), 0)
    hi_id = lax.broadcasted_iota(jnp.int32, (high, LANES), 0)

    def index(dev, j):
        return gbuf[0, dev, j:j + 1, :].astype(jnp.int32)

    def mark(dev, j):
        return jnp.where(lo_id == lax.rem(index(dev, j), py), 1.0, 0.0).astype(BF16)

    def hot(dev):
        for j in range(frows):
            onehot[dev, :, j * LANES:(j + 1) * LANES] = mark(dev, j)

    times(cols, hot)
    for j in range(frows):
        own_hot[:, j * LANES:(j + 1) * LANES] = mark(c, j)

    gather_wait(1)
    chunk = spread.shape[0]
    loads = jnp.zeros((3 * high, py), F32)
    for base in range(0, cols, chunk):
        def fill(dev):
            for j in range(frows):
                keep = hi_id == lax.div(index(base + dev, j), py)
                for part, v in enumerate(three(vbuf[base + dev, j:j + 1, :])):
                    tile = jnp.where(keep, v.astype(F32), 0.0).astype(BF16)
                    spread[dev, part * high:(part + 1) * high, j * LANES:(j + 1) * LANES] = tile

        times(chunk, fill)
        for dev in range(chunk):
            loads = loads + lax.dot_general(
                spread[dev], onehot[base + dev], NT, preferred_element_type=F32
            )
    slab = loads[:high] + loads[high:2 * high] + loads[2 * high:]
    for dev in range(cols):
        lslab[dev] = slab[dev * px:(dev + 1) * px]
    along_each(1, lambda copy: copy.start())

    halo_wait(2, (2, 3))
    for x in range(1, last):
        sweep(pa, pb, 2, x)
    halo_wait(2, (0, 1))
    for x in (0, last):
        sweep(pa, pb, 2, x)
    halo_start(3, (0, 1))
    pack(3)
    halo_start(3, (2, 3))

    along_each(0, lambda copy: copy.wait_recv(), back=True)
    tall, wide = lwin.shape
    win[:, WIN * px:, :] = jnp.zeros((3, tall - WIN * px, wide), F32)
    for w in range(WIN):
        for k in range(cols):
            for f in range(3):
                block = gbuf[1 + f, k] if w == NEAR else srecv[w, f, k]
                win[f, w * px:(w + 1) * px, k * py:(k + 1) * py] = block
    current, previous, thick = win[0], win[1], win[2]
    present = thick > 0.0
    inverse = jnp.where(present, 1.0 / jnp.where(present, thick, 1.0), 0.0)
    stiff = BEND * (thick * thick * thick)
    across = lax.broadcasted_iota(jnp.int32, (tall, wide), 1)

    def laplace(u):
        return (
            pltpu.roll(u, 1, 0) + pltpu.roll(u, tall - 1, 0)
            + jnp.where(across == 0, 0.0, pltpu.roll(u, 1, 1))
            + jnp.where(across == wide - 1, 0.0, pltpu.roll(u, wide - 1, 1)) - 4.0 * u
        )

    def free(now, before):
        return 2.0 * now - before - laplace(stiff * laplace(now)) * inverse

    ahead = free(current, previous)

    along_each(1, lambda copy: copy.wait_recv(), back=True)
    lwin[WIN * px:, :] = jnp.zeros((tall - WIN * px, wide), F32)
    for w in range(WIN):
        for k in range(cols):
            block = lslab[k] if w == NEAR else lrecv[w, k]
            lwin[w * px:(w + 1) * px, k * py:(k + 1) * py] = block
    push = LOADC * lwin[...] * inverse
    previous, current = current, ahead + push
    for _ in range(PSTEPS - 1):
        previous, current = current, free(current, previous) + push
    for dev in range(cols):
        piece = current[NEAR * px:(NEAR + 1) * px, dev * py:(dev + 1) * py]
        ubuf[dev] = piece
        uslab[dev * px:(dev + 1) * px, :] = piece
    plate_ref[...] = ubuf[c]

    parts = three(uslab[...])
    picked = lax.dot_general(
        jnp.concatenate(parts, axis=0), own_hot[...], (((1,), (0,)), ((), ())), preferred_element_type=F32
    )
    picked = picked[:high] + picked[high:2 * high] + picked[2 * high:]
    for j in range(frows):
        keep = hi_id == lax.div(index(c, j), py)
        part = jnp.where(keep, picked[:, j * LANES:(j + 1) * LANES], 0.0)
        motion_ref[j:j + 1, :] = jnp.sum(part, axis=0, keepdims=True)

    halo_wait(3, (2, 3))
    for x in range(1, last):
        sweep(pb, out_ref, 3, x)
    halo_wait(3, (0, 1))
    for x in (0, last):
        sweep(pb, out_ref, 3, x)

    for phase in range(4):
        halo_sent(phase)
    for dr, dc in blocks:
        @pl.when(both_ok(dr, dc))
        def _(dr=dr, dc=dc):
            skin(dr, dc).wait_send()
    for which in range(2):
        gather_sent(which)
        along_each(which, lambda copy: copy.wait_send())


def write(p_ref, plate_ref, motion_ref, p_out, plate_out, motion_out, sem):
    pairs = ((p_ref, p_out), (plate_ref, plate_out), (motion_ref, motion_out))
    copies = [pltpu.make_async_copy(a, b, sem.at[i]) for i, (a, b) in enumerate(pairs)]
    for copy in copies:
        copy.start()
    for copy in copies:
        copy.wait()


def shards(rows, cols, pressure, density, source, disp, prev, thick, owner, elem, wet):
    nx, ny, nz = pressure.shape
    px, py = disp.shape
    faces = elem.shape[0]
    frows = faces // LANES
    assert LANES == 2 * ny and nz == LANES and py == LANES
    high = cols * px
    tall = -(-WIN * px // 8) * 8
    chunk = 8 if cols % 8 == 0 else 1
    vmem = pl.BlockSpec(memory_space=pltpu.VMEM)
    hbm = pl.BlockSpec(memory_space=pltpu.HBM)
    dma = pltpu.SemaphoreType.DMA
    shapes = (
        jax.ShapeDtypeStruct(pressure.shape, F32),
        jax.ShapeDtypeStruct(disp.shape, F32),
        jax.ShapeDtypeStruct((frows, LANES), F32),
    )
    tables = [x.reshape(frows, LANES) for x in (owner, elem, wet)]
    operands = [
        pltpu.with_memory_space_constraint(x, pltpu.HBM)
        for x in (pressure, density, source, disp, prev, thick, *tables)
    ]
    results = pl.pallas_call(
        functools.partial(kernel, rows, cols),
        out_shape=tuple(pltpu.VMEM(s.shape, s.dtype) for s in shapes),
        in_specs=[hbm] * 9,
        out_specs=(vmem,) * 3,
        scratch_shapes=[
            pltpu.VMEM((nx, ny, nz), F32),
            pltpu.VMEM((nx, ny, nz), F32),
            pltpu.VMEM((nx, ny, nz), F32),
            pltpu.VMEM((3, px, py), F32),
            pltpu.VMEM((3, frows, LANES), jnp.int32),
            pltpu.VMEM((nx, ny, nz), F32),
            pltpu.VMEM((nx, ny, nz), F32),
            pltpu.VMEM((7, nx, ny, nz), F32),
            pltpu.VMEM((4, 2, ny, nz), F32),
            pltpu.VMEM((4, 2, nx, nz), F32),
            pltpu.VMEM((4, 2, nx, nz), F32),
            pltpu.VMEM((3, nx + 2 * SWEEPS, 8, LANES), F32),
            pltpu.VMEM((4, cols, px, py), F32),
            pltpu.VMEM((cols, frows, LANES), F32),
            pltpu.VMEM((cols, px, py), F32),
            pltpu.VMEM((WIN, 3, cols, px, py), F32),
            pltpu.VMEM((cols, px, py), F32),
            pltpu.VMEM((WIN, cols, px, py), F32),
            pltpu.VMEM((3, tall, cols * py), F32),
            pltpu.VMEM((tall, cols * py), F32),
            pltpu.VMEM((cols, py, faces), BF16),
            pltpu.VMEM((chunk, 3 * high, faces), BF16),
            pltpu.VMEM((py, faces), BF16),
            pltpu.VMEM((high, py), F32),
            dma((9,)),
            dma((4, 4)), dma((4, 4)),
            dma((2, cols - 1)), dma((2, cols - 1)),
            dma((9,)), dma((9,)),
            dma((2, WIN)), dma((2, WIN)),
        ],
        compiler_params=pltpu.CompilerParams(
            collective_id=0, has_side_effects=True, vmem_limit_bytes=48 * 1024 * 1024
        ),
        name="slamming",
    )(*operands)
    pressure, plate, motion = pl.pallas_call(
        write,
        out_shape=shapes,
        in_specs=[vmem] * 3,
        out_specs=(hbm,) * 3,
        scratch_shapes=[dma((3,))],
        compiler_params=pltpu.CompilerParams(vmem_limit_bytes=8 * 1024 * 1024),
        name="write_results",
    )(*results)
    return pressure, plate, motion.reshape(faces)


def solution(mesh):
    rows, cols = mesh.shape["row"], mesh.shape["col"]
    placed = (
        P("row", "col", None),
        P("row", "col", None),
        P("row", "col", None),
        P("row", "col"),
        P("row", "col"),
        P("row", "col"),
        P(("row", "col"), None),
        P(("row", "col")),
        P(("row", "col")),
    )
    return jax.shard_map(
        functools.partial(shards, rows, cols),
        mesh=mesh,
        in_specs=placed,
        out_specs=(P("row", "col", None), P("row", "col"), P(("row", "col"))),
        check_vma=False,
    )
```

```python
import functools

import jax
import jax.numpy as jnp
from jax import lax
from jax.experimental import pallas as pl
from jax.experimental.pallas import tpu as pltpu
from jax.sharding import PartitionSpec as P

SWEEPS = 3
PSTEPS = 4
OMEGA = 0.8
BEND = 0.006
LOADC = 0.25

LANES = 128
NEAR = 2
WIN = 2 * NEAR + 1
MESH = pl.DeviceIdType.MESH
NT = (((1,), (1,)), ((), ()))
F32 = jnp.float32
BF16 = jnp.bfloat16


def times(count, body):
    if count <= 32:
        for step in range(count):
            body(step)
    else:
        lax.fori_loop(0, count, lambda step, carry: (body(step), carry)[1], 0)


def three(value):
    a = value.astype(BF16)
    rest = value - a.astype(F32)
    b = rest.astype(BF16)
    c = (rest - b.astype(F32)).astype(BF16)
    return a, b, c


def kernel(
    rows, cols,
    p_hbm, c_hbm, s_hbm, disp_hbm, prev_hbm, thick_hbm, owner_hbm, elem_hbm, wet_hbm,
    out_ref, plate_ref, motion_ref,
    p_ref, c_ref, s_ref, small, faces_in,
    pa, pb, wt, xrecv, ysend, yrecv,
    thin, ibuf, vbuf, ubuf, stat, lslab, lrecv, win, lwin, onehot, spread, own_hot, uslab,
    lsem, fsend, frecv, gsend, grecv, tsend, trecv, rsend, rrecv,
):
    nx, ny, nz = p_ref.shape
    px, py = small.shape[1:]
    frows = faces_in.shape[1]
    high = cols * px
    last = nx - 1
    reach = SWEEPS
    r, c = lax.axis_index("row"), lax.axis_index("col")

    def row_ok(d):
        return jnp.logical_and(r + d >= 0, r + d < rows)

    def both_ok(dr, dc):
        return jnp.logical_and(row_ok(dr), jnp.logical_and(c + dc >= 0, c + dc < cols))

    shifts = [d for d in range(-NEAR, NEAR + 1) if d != 0]
    corners = [(dr, dc) for dr in (-1, 1) for dc in (-1, 1)]
    blocks = [(-1, 0), (1, 0), (0, -1), (0, 1)] + corners

    loads_in = [
        (c_hbm, c_ref), (p_hbm, p_ref), (s_hbm, s_ref),
        (disp_hbm, small.at[0]), (prev_hbm, small.at[1]), (thick_hbm, small.at[2]),
        (owner_hbm, faces_in.at[0]), (elem_hbm, faces_in.at[1]), (wet_hbm, faces_in.at[2]),
    ]
    loads_in = [pltpu.make_async_copy(a, b, lsem.at[i]) for i, (a, b) in enumerate(loads_in)]
    for copy in loads_in:
        copy.start()

    barrier = pltpu.get_barrier_semaphore()
    peers = cols - 1
    for dr, dc in [(d, 0) for d in shifts] + corners:
        @pl.when(both_ok(dr, dc))
        def _(dr=dr, dc=dc):
            pl.semaphore_signal(barrier, inc=1, device_id=(r + dr, c + dc), device_id_type=MESH)
        peers = peers + both_ok(dr, dc).astype(jnp.int32)

    def greet(step):
        pl.semaphore_signal(barrier, inc=1, device_id=(r, lax.rem(c + 1 + step, cols)), device_id_type=MESH)

    times(cols - 1, greet)

    gives = [r < rows - 1, r > 0, c < cols - 1, c > 0]
    takes = [r > 0, r < rows - 1, c > 0, c < cols - 1]
    fields = [c_ref, p_ref, pa, pb]
    sources = [c_hbm, p_hbm, pa, pb]

    def halo(phase, way):
        if way < 2:
            src = sources[phase].at[last if way == 0 else 0]
            dst = xrecv.at[phase, way]
            to = (r + 1 - 2 * way, c)
        else:
            src = ysend.at[phase, way - 2]
            dst = yrecv.at[phase, way - 2]
            to = (r, c + 1 - 2 * (way - 2))
        return pltpu.make_async_remote_copy(
            src_ref=src, dst_ref=dst, send_sem=fsend.at[phase, way], recv_sem=frecv.at[phase, way],
            device_id=to, device_id_type=MESH,
        )

    def halo_start(phase, ways):
        for way in ways:
            @pl.when(gives[way])
            def _(way=way):
                halo(phase, way).start()

    def halo_wait(phase, ways):
        for way in ways:
            @pl.when(takes[way])
            def _(way=way):
                halo(phase, way).wait_recv()

    def halo_sent(phase):
        for way in range(4):
            @pl.when(gives[way])
            def _(way=way):
                halo(phase, way).wait_send()

    def pack(phase):
        field = fields[phase]
        for x in range(nx):
            ysend[phase, 0, x:x + 1, :] = field[x, ny - 1:ny, :]
            ysend[phase, 1, x:x + 1, :] = field[x, 0:1, :]

    def slot(which, dev):
        return (ibuf, vbuf, stat)[which].at[dev]

    def gather(which, step):
        return pltpu.make_async_remote_copy(
            src_ref=slot(which, c), dst_ref=slot(which, c), send_sem=gsend.at[which, step],
            recv_sem=grecv.at[which, step], device_id=(r, lax.rem(c + 1 + step, cols)), device_id_type=MESH,
        )

    def gather_start(which):
        times(cols - 1, lambda step: gather(which, step).start())

    def gather_wait(which):
        def one(step):
            frm = lax.rem(c + cols - 1 - step, cols)
            pltpu.make_async_remote_copy(
                src_ref=slot(which, frm), dst_ref=slot(which, frm), send_sem=gsend.at[which, step],
                recv_sem=grecv.at[which, step], device_id=(r, frm), device_id_type=MESH,
            ).wait_recv()
        times(cols - 1, one)

    def gather_sent(which):
        times(cols - 1, lambda step: gather(which, step).wait_send())

    def along(which, d):
        src = stat.at[c, NEAR] if which == 0 else lslab
        dst = stat.at[c, NEAR - d] if which == 0 else lrecv.at[NEAR - d]
        return pltpu.make_async_remote_copy(
            src_ref=src, dst_ref=dst, send_sem=rsend.at[which, NEAR - d], recv_sem=rrecv.at[which, NEAR - d],
            device_id=(r + d, c), device_id_type=MESH,
        )

    def along_each(which, act, back=False):
        for d in shifts:
            @pl.when(row_ok(-d if back else d))
            def _(d=d):
                act(along(which, d))

    far = {-1: (0, reach), 0: (reach, nx), 1: (reach + nx, reach)}

    def skin(dr, dc):
        first = {-1: reach, 0: reach, 1: nx}[dr]
        at, count = far[-dr]
        return pltpu.make_async_remote_copy(
            src_ref=thin.at[1, pl.ds(first, count)], dst_ref=thin.at[1 - dc, pl.ds(at, count)],
            send_sem=tsend.at[3 * dr + dc + 4], recv_sem=trecv.at[3 * dr + dc + 4],
            device_id=(r + dr, c + dc), device_id_type=MESH,
        )

    for way in range(4):
        @pl.when(jnp.logical_not(takes[way]))
        def _(way=way):
            if way < 2:
                for phase in range(4):
                    xrecv[phase, way] = jnp.zeros((ny, nz), F32)
            else:
                for phase in range(4):
                    yrecv[phase, way - 2] = jnp.zeros((nx, nz), F32)
    for dr, dc in blocks:
        @pl.when(jnp.logical_not(both_ok(dr, dc)))
        def _(dr=dr, dc=dc):
            at, count = far[dr]
            thin[1 + dc, at:at + count] = jnp.zeros((count, 8, LANES), F32)
    for d in shifts:
        @pl.when(jnp.logical_not(row_ok(d)))
        def _(d=d):
            stat[c, NEAR + d] = jnp.zeros(stat.shape[2:], F32)
            lrecv[NEAR + d] = jnp.zeros(lrecv.shape[1:], F32)

    pl.semaphore_wait(barrier, peers)

    halo_start(0, (0, 1))
    halo_start(1, (0, 1))
    loads_in[0].wait()
    pack(0)
    halo_start(0, (2, 3))
    loads_in[1].wait()
    pack(1)
    halo_start(1, (2, 3))
    loads_in[2].wait()
    depth = lax.broadcasted_iota(jnp.int32, (8, nz), 0)
    layer = lax.broadcasted_iota(jnp.int32, (8, nz), 1)
    top = jnp.logical_and(depth == layer, depth < 4).astype(F32)
    low = (depth == layer + 4).astype(F32)

    def take(which, field):
        return lax.dot_general(
            which, field[...].reshape(nx * ny, nz), NT, precision=lax.Precision.HIGHEST,
            preferred_element_type=F32,
        )

    hull = take(top, p_ref) + take(low, c_ref)
    feed = take(top, s_ref)
    near = lax.broadcasted_iota(jnp.int32, (8, LANES), 1)
    for x in range(nx):
        v = (x // 2) * LANES
        one, two = hull[:, v:v + LANES], feed[:, v:v + LANES]
        if x % 2 == 0:
            two = pltpu.roll(two, ny, 1)
        else:
            one = pltpu.roll(one, ny, 1)
        thin[1, reach + x] = jnp.where(near < ny, one, two)
    for dr, dc in blocks:
        @pl.when(both_ok(dr, dc))
        def _(dr=dr, dc=dc):
            skin(dr, dc).start()
    for copy in loads_in[3:]:
        copy.wait()
    stat[c, NEAR] = small[...]
    along_each(0, lambda copy: copy.start())
    ibuf[c] = faces_in[0] * (px * py) + faces_in[1]
    gather_start(0)

    row_id = lax.broadcasted_iota(jnp.int32, (ny, nz), 0)
    lane_id = lax.broadcasted_iota(jnp.int32, (ny, nz), 1)

    def around(plane, phase, x):
        low = jnp.where(row_id == 0, yrecv[phase, 0, x:x + 1, :], pltpu.roll(plane, 1, 0))
        up = jnp.where(row_id == ny - 1, yrecv[phase, 1, x:x + 1, :], pltpu.roll(plane, ny - 1, 0))
        left = jnp.where(lane_id == 0, 0.0, pltpu.roll(plane, 1, 1))
        right = jnp.where(lane_id == nz - 1, 0.0, pltpu.roll(plane, nz - 1, 1))
        return low, up, left, right

    def beneath(field, phase, x):
        return (
            field[x - 1] if x > 0 else xrecv[phase, 0],
            field[x + 1] if x < last else xrecv[phase, 1],
        )

    def weights(mid, six):
        diag = 3.0 * mid + 0.5 * (((six[0] + six[1]) + (six[2] + six[3])) + (six[4] + six[5]))
        scale = OMEGA / diag
        half = 0.5 * scale
        return scale, [half * (mid + one) for one in six]

    def coefficients(x):
        mid = c_ref[x]
        scale, six = weights(mid, beneath(c_ref, 0, x) + around(mid, 0, x))
        wt[0, x] = scale * s_ref[x]
        for i in range(6):
            wt[1 + i, x] = six[i]

    def sweep(src, dst, phase, x):
        mid = src[x]
        six = beneath(src, phase, x) + around(mid, phase, x)
        total = (1.0 - OMEGA) * mid + wt[0, x]
        for i in range(6):
            total = total + wt[1 + i, x] * six[i]
        dst[x] = total

    halo_wait(0, (2, 3))
    for x in range(1, last):
        coefficients(x)
    halo_wait(1, (2, 3))
    for x in range(1, last):
        sweep(p_ref, pa, 1, x)

    for dr, dc in blocks:
        @pl.when(both_ok(-dr, -dc))
        def _(dr=dr, dc=dc):
            skin(dr, dc).wait_recv()
    half = ny // 2
    ps, cs, ss = [], [], []
    for x in range(nx + 2 * reach):
        left, own, right = thin[0, x], thin[1, x], thin[2, x]
        side = jnp.where(near >= half, left, right)
        middle = jnp.logical_and(near >= half, near < half + ny)
        pc = jnp.where(middle, pltpu.roll(own, half, 1), pltpu.roll(side, half + ny, 1))
        side = jnp.where(near >= ny + half, left, right)
        ss.append(jnp.where(middle, pltpu.roll(own, half + ny, 1), pltpu.roll(side, half, 1)))
        ps.append(jnp.where(depth[:, :LANES] < 4, pc, 0.0))
        cs.append(jnp.where(depth[:, :LANES] < 4, pltpu.roll(pc, 4, 0), 0.0))

    def thin_six(field, x):
        mid = field[x]
        return (
            field[x - 1], field[x + 1], pltpu.roll(mid, 1, 1), pltpu.roll(mid, LANES - 1, 1),
            jnp.where(depth == 0, 0.0, pltpu.roll(mid, 1, 0)), pltpu.roll(mid, 7, 0),
        )

    shares = {}
    for x in range(1, nx + 2 * reach - 1):
        scale, six = weights(cs[x], thin_six(cs, x))
        shares[x] = (scale * ss[x], six, cs[x] > 0.0)
    for level in range(1, reach + 1):
        new = list(ps)
        for x in range(level, nx + 2 * reach - level):
            fixed, six, inside = shares[x]
            total = (1.0 - OMEGA) * ps[x] + fixed
            for a, b in zip(six, thin_six(ps, x)):
                total = total + a * b
            new[x] = jnp.where(inside, total, 0.0)
        ps = new
    for j in range(frows):
        even = pltpu.roll(ps[reach + 2 * j], LANES - half, 1)
        odd = pltpu.roll(ps[reach + 2 * j + 1], half, 1)
        face = jnp.where(near < ny, even, odd)[0:1]
        vbuf[c, j:j + 1, :] = face * faces_in[2, j:j + 1, :].astype(F32)
    gather_start(1)

    halo_wait(0, (0, 1))
    for x in (0, last):
        coefficients(x)
    halo_wait(1, (0, 1))
    for x in (0, last):
        sweep(p_ref, pa, 1, x)
    halo_start(2, (0, 1))
    pack(2)
    halo_start(2, (2, 3))

    along_each(0, lambda copy: copy.wait_recv(), back=True)
    gather_start(2)
    gather_wait(0)
    lo_id = lax.broadcasted_iota(jnp.int32, (py, LANES), 0)
    hi_id = lax.broadcasted_iota(jnp.int32, (high, LANES), 0)

    def index(dev, j):
        return ibuf[dev, j:j + 1, :]

    def mark(dev, j):
        return jnp.where(lo_id == lax.rem(index(dev, j), py), 1.0, 0.0).astype(BF16)

    def hot(dev):
        for j in range(frows):
            onehot[dev, :, j * LANES:(j + 1) * LANES] = mark(dev, j)

    times(cols, hot)
    for j in range(frows):
        own_hot[:, j * LANES:(j + 1) * LANES] = mark(c, j)

    halo_wait(2, (0, 1, 2, 3))
    for x in (0, last):
        sweep(pa, pb, 2, x)
    halo_start(3, (0, 1))
    for x in range(1, last):
        sweep(pa, pb, 2, x)
    pack(3)
    halo_start(3, (2, 3))

    gather_wait(1)
    chunk = spread.shape[0]
    loads = jnp.zeros((3 * high, py), F32)
    for base in range(0, cols, chunk):
        def fill(dev):
            for j in range(frows):
                keep = hi_id == lax.div(index(base + dev, j), py)
                for part, v in enumerate(three(vbuf[base + dev, j:j + 1, :])):
                    tile = jnp.where(keep, v.astype(F32), 0.0).astype(BF16)
                    spread[dev, part * high:(part + 1) * high, j * LANES:(j + 1) * LANES] = tile

        times(chunk, fill)
        for dev in range(chunk):
            loads = loads + lax.dot_general(
                spread[dev], onehot[base + dev], NT, preferred_element_type=F32
            )
    slab = loads[:high] + loads[high:2 * high] + loads[2 * high:]
    for dev in range(cols):
        lslab[dev] = slab[dev * px:(dev + 1) * px]
    along_each(1, lambda copy: copy.start())

    gather_wait(2)
    tall, wide = lwin.shape
    win[:, WIN * px:, :] = jnp.zeros((3, tall - WIN * px, wide), F32)
    for w in range(WIN):
        for k in range(cols):
            for f in range(3):
                win[f, w * px:(w + 1) * px, k * py:(k + 1) * py] = stat[k, w, f]
    current, previous, thick = win[0], win[1], win[2]
    present = thick > 0.0
    inverse = jnp.where(present, 1.0 / jnp.where(present, thick, 1.0), 0.0)
    stiff = BEND * (thick * thick * thick)
    across = lax.broadcasted_iota(jnp.int32, (tall, wide), 1)

    def laplace(u):
        return (
            pltpu.roll(u, 1, 0) + pltpu.roll(u, tall - 1, 0)
            + jnp.where(across == 0, 0.0, pltpu.roll(u, 1, 1))
            + jnp.where(across == wide - 1, 0.0, pltpu.roll(u, wide - 1, 1)) - 4.0 * u
        )

    def free(now, before):
        return 2.0 * now - before - laplace(stiff * laplace(now)) * inverse

    ahead = free(current, previous)

    halo_wait(3, (2, 3))
    for x in range(1, last):
        sweep(pb, out_ref, 3, x)

    for phase in range(3):
        halo_sent(phase)
    for dr, dc in blocks:
        @pl.when(both_ok(dr, dc))
        def _(dr=dr, dc=dc):
            skin(dr, dc).wait_send()
    for which in range(3):
        gather_sent(which)
    along_each(0, lambda copy: copy.wait_send())

    along_each(1, lambda copy: copy.wait_recv(), back=True)
    lwin[WIN * px:, :] = jnp.zeros((tall - WIN * px, wide), F32)
    for w in range(WIN):
        for k in range(cols):
            block = lslab[k] if w == NEAR else lrecv[w, k]
            lwin[w * px:(w + 1) * px, k * py:(k + 1) * py] = block
    push = LOADC * lwin[...] * inverse
    previous, current = current, ahead + push
    for _ in range(PSTEPS - 1):
        previous, current = current, free(current, previous) + push
    for dev in range(cols):
        piece = current[NEAR * px:(NEAR + 1) * px, dev * py:(dev + 1) * py]
        ubuf[dev] = piece
        uslab[dev * px:(dev + 1) * px, :] = piece
    plate_ref[...] = ubuf[c]

    parts = three(uslab[...])
    picked = lax.dot_general(
        jnp.concatenate(parts, axis=0), own_hot[...], (((1,), (0,)), ((), ())), preferred_element_type=F32
    )
    picked = picked[:high] + picked[high:2 * high] + picked[2 * high:]
    for j in range(frows):
        keep = hi_id == lax.div(index(c, j), py)
        part = jnp.where(keep, picked[:, j * LANES:(j + 1) * LANES], 0.0)
        motion_ref[j:j + 1, :] = jnp.sum(part, axis=0, keepdims=True)

    halo_wait(3, (0, 1))
    for x in (0, last):
        sweep(pb, out_ref, 3, x)
    halo_sent(3)
    along_each(1, lambda copy: copy.wait_send())


def write(p_ref, plate_ref, motion_ref, p_out, plate_out, motion_out, sem):
    pairs = ((p_ref, p_out), (plate_ref, plate_out), (motion_ref, motion_out))
    copies = [pltpu.make_async_copy(a, b, sem.at[i]) for i, (a, b) in enumerate(pairs)]
    for copy in copies:
        copy.start()
    for copy in copies:
        copy.wait()


def shards(rows, cols, pressure, density, source, disp, prev, thick, owner, elem, wet):
    nx, ny, nz = pressure.shape
    px, py = disp.shape
    faces = elem.shape[0]
    frows = faces // LANES
    assert LANES == 2 * ny and nz == LANES and py == LANES
    high = cols * px
    tall = -(-WIN * px // 8) * 8
    chunk = 8 if cols % 8 == 0 else 1
    vmem = pl.BlockSpec(memory_space=pltpu.VMEM)
    hbm = pl.BlockSpec(memory_space=pltpu.HBM)
    dma = pltpu.SemaphoreType.DMA
    shapes = (
        jax.ShapeDtypeStruct(pressure.shape, F32),
        jax.ShapeDtypeStruct(disp.shape, F32),
        jax.ShapeDtypeStruct((frows, LANES), F32),
    )
    tables = [x.reshape(frows, LANES) for x in (owner, elem, wet)]
    operands = [
        pltpu.with_memory_space_constraint(x, pltpu.HBM)
        for x in (pressure, density, source, disp, prev, thick, *tables)
    ]
    results = pl.pallas_call(
        functools.partial(kernel, rows, cols),
        out_shape=tuple(pltpu.VMEM(s.shape, s.dtype) for s in shapes),
        in_specs=[hbm] * 9,
        out_specs=(vmem,) * 3,
        scratch_shapes=[
            pltpu.VMEM((nx, ny, nz), F32),
            pltpu.VMEM((nx, ny, nz), F32),
            pltpu.VMEM((nx, ny, nz), F32),
            pltpu.VMEM((3, px, py), F32),
            pltpu.VMEM((3, frows, LANES), jnp.int32),
            pltpu.VMEM((nx, ny, nz), F32),
            pltpu.VMEM((nx, ny, nz), F32),
            pltpu.VMEM((7, nx, ny, nz), F32),
            pltpu.VMEM((4, 2, ny, nz), F32),
            pltpu.VMEM((4, 2, nx, nz), F32),
            pltpu.VMEM((4, 2, nx, nz), F32),
            pltpu.VMEM((3, nx + 2 * SWEEPS, 8, LANES), F32),
            pltpu.VMEM((cols, frows, LANES), jnp.int32),
            pltpu.VMEM((cols, frows, LANES), F32),
            pltpu.VMEM((cols, px, py), F32),
            pltpu.VMEM((cols, WIN, 3, px, py), F32),
            pltpu.VMEM((cols, px, py), F32),
            pltpu.VMEM((WIN, cols, px, py), F32),
            pltpu.VMEM((3, tall, cols * py), F32),
            pltpu.VMEM((tall, cols * py), F32),
            pltpu.VMEM((cols, py, faces), BF16),
            pltpu.VMEM((chunk, 3 * high, faces), BF16),
            pltpu.VMEM((py, faces), BF16),
            pltpu.VMEM((high, py), F32),
            dma((9,)),
            dma((4, 4)), dma((4, 4)),
            dma((3, cols - 1)), dma((3, cols - 1)),
            dma((9,)), dma((9,)),
            dma((2, WIN)), dma((2, WIN)),
        ],
        compiler_params=pltpu.CompilerParams(
            collective_id=0, has_side_effects=True, vmem_limit_bytes=48 * 1024 * 1024
        ),
        name="slamming",
    )(*operands)
    pressure, plate, motion = pl.pallas_call(
        write,
        out_shape=shapes,
        in_specs=[vmem] * 3,
        out_specs=(hbm,) * 3,
        scratch_shapes=[dma((3,))],
        compiler_params=pltpu.CompilerParams(vmem_limit_bytes=8 * 1024 * 1024),
        name="write_results",
    )(*results)
    return pressure, plate, motion.reshape(faces)


def solution(mesh):
    rows, cols = mesh.shape["row"], mesh.shape["col"]
    placed = (
        P("row", "col", None),
        P("row", "col", None),
        P("row", "col", None),
        P("row", "col"),
        P("row", "col"),
        P("row", "col"),
        P(("row", "col"), None),
        P(("row", "col")),
        P(("row", "col")),
    )
    return jax.shard_map(
        functools.partial(shards, rows, cols),
        mesh=mesh,
        in_specs=placed,
        out_specs=(P("row", "col", None), P("row", "col"), P(("row", "col"))),
        check_vma=False,
    )
```

```python
import functools

import jax
import jax.numpy as jnp
from jax import lax
from jax.experimental import pallas as pl
from jax.experimental.pallas import tpu as pltpu
from jax.sharding import PartitionSpec as P

SWEEPS = 3
PSTEPS = 4
OMEGA = 0.8
BEND = 0.006
LOADC = 0.25

LANES = 128
NEAR = 2
WIN = 2 * NEAR + 1
MESH = pl.DeviceIdType.MESH
NT = (((1,), (1,)), ((), ()))
F32 = jnp.float32
BF16 = jnp.bfloat16


def times(count, body):
    if count <= 32:
        for step in range(count):
            body(step)
    else:
        lax.fori_loop(0, count, lambda step, carry: (body(step), carry)[1], 0)


def three(value):
    a = value.astype(BF16)
    rest = value - a.astype(F32)
    b = rest.astype(BF16)
    c = (rest - b.astype(F32)).astype(BF16)
    return a, b, c


def kernel(
    rows, cols,
    p_hbm, c_hbm, s_hbm, disp_hbm, prev_hbm, thick_hbm, owner_hbm, elem_hbm, wet_hbm,
    out_ref, plate_ref, motion_ref,
    p_ref, c_ref, s_ref, small, faces_in,
    pa, pb, wt, xrecv, ysend, yrecv,
    strip, thin, gbuf, vbuf, ubuf, srecv, lslab, lrecv, win, lwin, onehot, spread, own_hot, uslab,
    lsem, fsend, frecv, gsend, grecv, tsend, trecv, rsend, rrecv,
):
    nx, ny, nz = p_ref.shape
    px, py = small.shape[1:]
    frows = faces_in.shape[1]
    high = cols * px
    last = nx - 1
    reach = SWEEPS
    r, c = lax.axis_index("row"), lax.axis_index("col")

    def row_ok(d):
        return jnp.logical_and(r + d >= 0, r + d < rows)

    def both_ok(dr, dc):
        return jnp.logical_and(row_ok(dr), jnp.logical_and(c + dc >= 0, c + dc < cols))

    shifts = [d for d in range(-NEAR, NEAR + 1) if d != 0]
    corners = [(dr, dc) for dr in (-1, 1) for dc in (-1, 1)]
    blocks = [(-1, 0), (1, 0), (0, -1), (0, 1)] + corners

    loads_in = [
        (c_hbm, c_ref), (p_hbm, p_ref), (s_hbm, s_ref),
        (disp_hbm, small.at[0]), (prev_hbm, small.at[1]), (thick_hbm, small.at[2]),
        (owner_hbm, faces_in.at[0]), (elem_hbm, faces_in.at[1]), (wet_hbm, faces_in.at[2]),
    ]
    loads_in = [pltpu.make_async_copy(a, b, lsem.at[i]) for i, (a, b) in enumerate(loads_in)]
    for copy in loads_in:
        copy.start()

    barrier = pltpu.get_barrier_semaphore()
    peers = cols - 1
    for dr, dc in [(d, 0) for d in shifts] + corners:
        @pl.when(both_ok(dr, dc))
        def _(dr=dr, dc=dc):
            pl.semaphore_signal(barrier, inc=1, device_id=(r + dr, c + dc), device_id_type=MESH)
        peers = peers + both_ok(dr, dc).astype(jnp.int32)

    def greet(step):
        pl.semaphore_signal(barrier, inc=1, device_id=(r, lax.rem(c + 1 + step, cols)), device_id_type=MESH)

    times(cols - 1, greet)

    gives = [r < rows - 1, r > 0, c < cols - 1, c > 0]
    takes = [r > 0, r < rows - 1, c > 0, c < cols - 1]
    fields = [c_ref, p_ref, pa, pb]

    def halo(phase, way):
        if way < 2:
            src = fields[phase].at[last if way == 0 else 0]
            dst = xrecv.at[phase, way]
            to = (r + 1 - 2 * way, c)
        else:
            src = ysend.at[phase, way - 2]
            dst = yrecv.at[phase, way - 2]
            to = (r, c + 1 - 2 * (way - 2))
        return pltpu.make_async_remote_copy(
            src_ref=src, dst_ref=dst, send_sem=fsend.at[phase, way], recv_sem=frecv.at[phase, way],
            device_id=to, device_id_type=MESH,
        )

    def halo_start(phase, ways):
        for way in ways:
            @pl.when(gives[way])
            def _(way=way):
                halo(phase, way).start()

    def halo_wait(phase, ways):
        for way in ways:
            @pl.when(takes[way])
            def _(way=way):
                halo(phase, way).wait_recv()

    def halo_sent(phase):
        for way in range(4):
            @pl.when(gives[way])
            def _(way=way):
                halo(phase, way).wait_send()

    def pack(phase):
        field = fields[phase]
        for x in range(nx):
            ysend[phase, 0, x:x + 1, :] = field[x, ny - 1:ny, :]
            ysend[phase, 1, x:x + 1, :] = field[x, 0:1, :]

    def slot(which, dev):
        return gbuf.at[:, dev] if which == 0 else vbuf.at[dev]

    def gather(which, step):
        return pltpu.make_async_remote_copy(
            src_ref=slot(which, c), dst_ref=slot(which, c), send_sem=gsend.at[which, step],
            recv_sem=grecv.at[which, step], device_id=(r, lax.rem(c + 1 + step, cols)), device_id_type=MESH,
        )

    def gather_start(which):
        times(cols - 1, lambda step: gather(which, step).start())

    def gather_wait(which):
        def one(step):
            frm = lax.rem(c + cols - 1 - step, cols)
            pltpu.make_async_remote_copy(
                src_ref=slot(which, frm), dst_ref=slot(which, frm), send_sem=gsend.at[which, step],
                recv_sem=grecv.at[which, step], device_id=(r, frm), device_id_type=MESH,
            ).wait_recv()
        times(cols - 1, one)

    def gather_sent(which):
        times(cols - 1, lambda step: gather(which, step).wait_send())

    def along(which, d):
        src = gbuf.at[pl.ds(1, 3)] if which == 0 else lslab
        dst = (srecv if which == 0 else lrecv).at[NEAR - d]
        return pltpu.make_async_remote_copy(
            src_ref=src, dst_ref=dst, send_sem=rsend.at[which, NEAR - d], recv_sem=rrecv.at[which, NEAR - d],
            device_id=(r + d, c), device_id_type=MESH,
        )

    def along_each(which, act, back=False):
        for d in shifts:
            @pl.when(row_ok(-d if back else d))
            def _(d=d):
                act(along(which, d))

    far = {-1: (0, reach), 0: (reach, nx), 1: (reach + nx, reach)}

    def skin(dr, dc):
        first = {-1: reach, 0: reach, 1: nx}[dr]
        at, count = far[-dr]
        return pltpu.make_async_remote_copy(
            src_ref=thin.at[1, pl.ds(first, count)], dst_ref=thin.at[1 - dc, pl.ds(at, count)],
            send_sem=tsend.at[3 * dr + dc + 4], recv_sem=trecv.at[3 * dr + dc + 4],
            device_id=(r + dr, c + dc), device_id_type=MESH,
        )

    for way in range(4):
        @pl.when(jnp.logical_not(takes[way]))
        def _(way=way):
            if way < 2:
                for phase in range(4):
                    xrecv[phase, way] = jnp.zeros((ny, nz), F32)
            else:
                for phase in range(4):
                    yrecv[phase, way - 2] = jnp.zeros((nx, nz), F32)
    for dr, dc in blocks:
        @pl.when(jnp.logical_not(both_ok(dr, dc)))
        def _(dr=dr, dc=dc):
            at, count = far[dr]
            thin[1 + dc, at:at + count] = jnp.zeros((count, 8, LANES), F32)
    for d in shifts:
        @pl.when(jnp.logical_not(row_ok(d)))
        def _(d=d):
            srecv[NEAR + d] = jnp.zeros(srecv.shape[1:], F32)
            lrecv[NEAR + d] = jnp.zeros(lrecv.shape[1:], F32)

    for copy in loads_in[:3]:
        copy.wait()
    depth = lax.broadcasted_iota(jnp.int32, (8, LANES), 0)
    along_z = lax.broadcasted_iota(jnp.int32, (ny, nz), 1)
    for x in range(nx):
        layers = jnp.where(
            along_z < 4, p_ref[x], jnp.where(along_z < 8, pltpu.roll(c_ref[x], 4, 1), pltpu.roll(s_ref[x], 8, 1))
        )
        for part, value in enumerate(three(layers)):
            strip[part, x * ny:(x + 1) * ny, :] = value
    pick = jnp.where(
        lax.broadcasted_iota(jnp.int32, (16, nz), 0) == lax.broadcasted_iota(jnp.int32, (16, nz), 1), 1.0, 0.0
    ).astype(BF16)
    moved = [lax.dot_general(pick, strip[part], NT, preferred_element_type=F32) for part in range(3)]
    moved = (moved[0] + moved[1]) + moved[2]
    hull, feed = moved[:8], moved[8:]
    near = lax.broadcasted_iota(jnp.int32, (8, LANES), 1)
    for x in range(nx):
        v = (x // 2) * LANES
        one, two = hull[:, v:v + LANES], feed[:, v:v + LANES]
        if x % 2 == 0:
            two = pltpu.roll(two, ny, 1)
        else:
            one = pltpu.roll(one, ny, 1)
        thin[1, reach + x] = jnp.where(near < ny, one, two)

    pl.semaphore_wait(barrier, peers)

    for dr, dc in blocks:
        @pl.when(both_ok(dr, dc))
        def _(dr=dr, dc=dc):
            skin(dr, dc).start()
    halo_start(0, (0, 1))
    halo_start(1, (0, 1))
    pack(0)
    halo_start(0, (2, 3))
    pack(1)
    halo_start(1, (2, 3))
    for copy in loads_in[3:]:
        copy.wait()
    gbuf[0, c] = (faces_in[0] * (px * py) + faces_in[1]).astype(F32)
    for f in range(3):
        gbuf[1 + f, c] = small[f]
    gather_start(0)

    row_id = lax.broadcasted_iota(jnp.int32, (ny, nz), 0)
    lane_id = lax.broadcasted_iota(jnp.int32, (ny, nz), 1)

    def around(plane, phase, x):
        low = jnp.where(row_id == 0, yrecv[phase, 0, x:x + 1, :], pltpu.roll(plane, 1, 0))
        up = jnp.where(row_id == ny - 1, yrecv[phase, 1, x:x + 1, :], pltpu.roll(plane, ny - 1, 0))
        left = jnp.where(lane_id == 0, 0.0, pltpu.roll(plane, 1, 1))
        right = jnp.where(lane_id == nz - 1, 0.0, pltpu.roll(plane, nz - 1, 1))
        return low, up, left, right

    def beneath(field, phase, x):
        return (
            field[x - 1] if x > 0 else xrecv[phase, 0],
            field[x + 1] if x < last else xrecv[phase, 1],
        )

    def weights(mid, six):
        diag = 3.0 * mid + 0.5 * (((six[0] + six[1]) + (six[2] + six[3])) + (six[4] + six[5]))
        scale = OMEGA / diag
        half = 0.5 * scale
        return scale, [half * (mid + one) for one in six]

    def coefficients(x):
        mid = c_ref[x]
        scale, six = weights(mid, beneath(c_ref, 0, x) + around(mid, 0, x))
        wt[0, x] = scale * s_ref[x]
        for i in range(6):
            wt[1 + i, x] = six[i]

    def sweep(src, dst, phase, x):
        mid = src[x]
        six = beneath(src, phase, x) + around(mid, phase, x)
        total = (1.0 - OMEGA) * mid + wt[0, x]
        for i in range(6):
            total = total + wt[1 + i, x] * six[i]
        dst[x] = total

    halo_wait(0, (2, 3))
    for x in range(1, last):
        coefficients(x)
    halo_wait(1, (2, 3))
    for x in range(1, last):
        sweep(p_ref, pa, 1, x)

    for dr, dc in blocks:
        @pl.when(both_ok(-dr, -dc))
        def _(dr=dr, dc=dc):
            skin(dr, dc).wait_recv()
    half = ny // 2
    ps, cs, ss = [], [], []
    for x in range(nx + 2 * reach):
        left, own, right = thin[0, x], thin[1, x], thin[2, x]
        side = jnp.where(near >= half, left, right)
        middle = jnp.logical_and(near >= half, near < half + ny)
        pc = jnp.where(middle, pltpu.roll(own, half, 1), pltpu.roll(side, half + ny, 1))
        side = jnp.where(near >= ny + half, left, right)
        ss.append(jnp.where(middle, pltpu.roll(own, half + ny, 1), pltpu.roll(side, half, 1)))
        ps.append(jnp.where(depth < 4, pc, 0.0))
        cs.append(jnp.where(depth < 4, pltpu.roll(pc, 4, 0), 0.0))

    def thin_six(field, x):
        mid = field[x]
        return (
            field[x - 1], field[x + 1], pltpu.roll(mid, 1, 1), pltpu.roll(mid, LANES - 1, 1),
            jnp.where(depth == 0, 0.0, pltpu.roll(mid, 1, 0)), pltpu.roll(mid, 7, 0),
        )

    shares = {}
    for x in range(1, nx + 2 * reach - 1):
        scale, six = weights(cs[x], thin_six(cs, x))
        shares[x] = (scale * ss[x], six, cs[x] > 0.0)
    for level in range(1, reach + 1):
        new = list(ps)
        for x in range(level, nx + 2 * reach - level):
            fixed, six, inside = shares[x]
            total = (1.0 - OMEGA) * ps[x] + fixed
            for a, b in zip(six, thin_six(ps, x)):
                total = total + a * b
            new[x] = jnp.where(inside, total, 0.0)
        ps = new
    for j in range(frows):
        even = pltpu.roll(ps[reach + 2 * j], LANES - half, 1)
        odd = pltpu.roll(ps[reach + 2 * j + 1], half, 1)
        face = jnp.where(near < ny, even, odd)[0:1]
        vbuf[c, j:j + 1, :] = face * faces_in[2, j:j + 1, :].astype(F32)
    gather_start(1)

    halo_wait(0, (0, 1))
    for x in (0, last):
        coefficients(x)
    halo_wait(1, (0, 1))
    for x in (0, last):
        sweep(p_ref, pa, 1, x)
    halo_start(2, (0, 1))
    pack(2)
    halo_start(2, (2, 3))

    gather_wait(0)
    along_each(0, lambda copy: copy.start())
    lo_id = lax.broadcasted_iota(jnp.int32, (py, LANES), 0)
    hi_id = lax.broadcasted_iota(jnp.int32, (high, LANES), 0)

    def index(dev, j):
        return gbuf[0, dev, j:j + 1, :].astype(jnp.int32)

    def mark(dev, j):
        return jnp.where(lo_id == lax.rem(index(dev, j), py), 1.0, 0.0).astype(BF16)

    def hot(dev):
        for j in range(frows):
            onehot[dev, :, j * LANES:(j + 1) * LANES] = mark(dev, j)

    times(cols, hot)
    for j in range(frows):
        own_hot[:, j * LANES:(j + 1) * LANES] = mark(c, j)

    gather_wait(1)
    chunk = spread.shape[0]
    loads = jnp.zeros((3 * high, py), F32)
    for base in range(0, cols, chunk):
        def fill(dev):
            for j in range(frows):
                keep = hi_id == lax.div(index(base + dev, j), py)
                for part, v in enumerate(three(vbuf[base + dev, j:j + 1, :])):
                    tile = jnp.where(keep, v.astype(F32), 0.0).astype(BF16)
                    spread[dev, part * high:(part + 1) * high, j * LANES:(j + 1) * LANES] = tile

        times(chunk, fill)
        for dev in range(chunk):
            loads = loads + lax.dot_general(
                spread[dev], onehot[base + dev], NT, preferred_element_type=F32
            )
    slab = loads[:high] + loads[high:2 * high] + loads[2 * high:]
    for dev in range(cols):
        lslab[dev] = slab[dev * px:(dev + 1) * px]
    along_each(1, lambda copy: copy.start())

    halo_wait(2, (0, 1, 2, 3))
    for x in (0, last):
        sweep(pa, pb, 2, x)
    halo_start(3, (0, 1))
    for x in range(1, last):
        sweep(pa, pb, 2, x)
    pack(3)
    halo_start(3, (2, 3))

    along_each(0, lambda copy: copy.wait_recv(), back=True)
    tall, wide = lwin.shape
    win[:, WIN * px:, :] = jnp.zeros((3, tall - WIN * px, wide), F32)
    for w in range(WIN):
        for k in range(cols):
            for f in range(3):
                block = gbuf[1 + f, k] if w == NEAR else srecv[w, f, k]
                win[f, w * px:(w + 1) * px, k * py:(k + 1) * py] = block
    current, previous, thick = win[0], win[1], win[2]
    present = thick > 0.0
    inverse = jnp.where(present, 1.0 / jnp.where(present, thick, 1.0), 0.0)
    stiff = BEND * (thick * thick * thick)
    across = lax.broadcasted_iota(jnp.int32, (tall, wide), 1)

    def laplace(u):
        return (
            pltpu.roll(u, 1, 0) + pltpu.roll(u, tall - 1, 0)
            + jnp.where(across == 0, 0.0, pltpu.roll(u, 1, 1))
            + jnp.where(across == wide - 1, 0.0, pltpu.roll(u, wide - 1, 1)) - 4.0 * u
        )

    def free(now, before):
        return 2.0 * now - before - laplace(stiff * laplace(now)) * inverse

    ahead = free(current, previous)

    halo_wait(3, (2, 3))
    for x in range(1, last):
        sweep(pb, out_ref, 3, x)

    for phase in range(3):
        halo_sent(phase)
    for dr, dc in blocks:
        @pl.when(both_ok(dr, dc))
        def _(dr=dr, dc=dc):
            skin(dr, dc).wait_send()
    for which in range(2):
        gather_sent(which)
    along_each(0, lambda copy: copy.wait_send())

    along_each(1, lambda copy: copy.wait_recv(), back=True)
    lwin[WIN * px:, :] = jnp.zeros((tall - WIN * px, wide), F32)
    for w in range(WIN):
        for k in range(cols):
            block = lslab[k] if w == NEAR else lrecv[w, k]
            lwin[w * px:(w + 1) * px, k * py:(k + 1) * py] = block
    push = LOADC * lwin[...] * inverse
    previous, current = current, ahead + push
    for _ in range(PSTEPS - 1):
        previous, current = current, free(current, previous) + push
    for dev in range(cols):
        piece = current[NEAR * px:(NEAR + 1) * px, dev * py:(dev + 1) * py]
        ubuf[dev] = piece
        uslab[dev * px:(dev + 1) * px, :] = piece
    plate_ref[...] = ubuf[c]

    parts = three(uslab[...])
    picked = lax.dot_general(
        jnp.concatenate(parts, axis=0), own_hot[...], (((1,), (0,)), ((), ())), preferred_element_type=F32
    )
    picked = picked[:high] + picked[high:2 * high] + picked[2 * high:]
    for j in range(frows):
        keep = hi_id == lax.div(index(c, j), py)
        part = jnp.where(keep, picked[:, j * LANES:(j + 1) * LANES], 0.0)
        motion_ref[j:j + 1, :] = jnp.sum(part, axis=0, keepdims=True)

    halo_wait(3, (0, 1))
    for x in (0, last):
        sweep(pb, out_ref, 3, x)
    halo_sent(3)
    along_each(1, lambda copy: copy.wait_send())


def write(p_ref, plate_ref, motion_ref, p_out, plate_out, motion_out, sem):
    pairs = ((p_ref, p_out), (plate_ref, plate_out), (motion_ref, motion_out))
    copies = [pltpu.make_async_copy(a, b, sem.at[i]) for i, (a, b) in enumerate(pairs)]
    for copy in copies:
        copy.start()
    for copy in copies:
        copy.wait()


def shards(rows, cols, pressure, density, source, disp, prev, thick, owner, elem, wet):
    nx, ny, nz = pressure.shape
    px, py = disp.shape
    faces = elem.shape[0]
    frows = faces // LANES
    assert LANES == 2 * ny and nz == LANES and py == LANES
    high = cols * px
    tall = -(-WIN * px // 8) * 8
    chunk = 8 if cols % 8 == 0 else 1
    vmem = pl.BlockSpec(memory_space=pltpu.VMEM)
    hbm = pl.BlockSpec(memory_space=pltpu.HBM)
    dma = pltpu.SemaphoreType.DMA
    shapes = (
        jax.ShapeDtypeStruct(pressure.shape, F32),
        jax.ShapeDtypeStruct(disp.shape, F32),
        jax.ShapeDtypeStruct((frows, LANES), F32),
    )
    tables = [x.reshape(frows, LANES) for x in (owner, elem, wet)]
    operands = [
        pltpu.with_memory_space_constraint(x, pltpu.HBM)
        for x in (pressure, density, source, disp, prev, thick, *tables)
    ]
    results = pl.pallas_call(
        functools.partial(kernel, rows, cols),
        out_shape=tuple(pltpu.VMEM(s.shape, s.dtype) for s in shapes),
        in_specs=[hbm] * 9,
        out_specs=(vmem,) * 3,
        scratch_shapes=[
            pltpu.VMEM((nx, ny, nz), F32),
            pltpu.VMEM((nx, ny, nz), F32),
            pltpu.VMEM((nx, ny, nz), F32),
            pltpu.VMEM((3, px, py), F32),
            pltpu.VMEM((3, frows, LANES), jnp.int32),
            pltpu.VMEM((nx, ny, nz), F32),
            pltpu.VMEM((nx, ny, nz), F32),
            pltpu.VMEM((7, nx, ny, nz), F32),
            pltpu.VMEM((4, 2, ny, nz), F32),
            pltpu.VMEM((4, 2, nx, nz), F32),
            pltpu.VMEM((4, 2, nx, nz), F32),
            pltpu.VMEM((3, nx * ny, nz), BF16),
            pltpu.VMEM((3, nx + 2 * SWEEPS, 8, LANES), F32),
            pltpu.VMEM((4, cols, px, py), F32),
            pltpu.VMEM((cols, frows, LANES), F32),
            pltpu.VMEM((cols, px, py), F32),
            pltpu.VMEM((WIN, 3, cols, px, py), F32),
            pltpu.VMEM((cols, px, py), F32),
            pltpu.VMEM((WIN, cols, px, py), F32),
            pltpu.VMEM((3, tall, cols * py), F32),
            pltpu.VMEM((tall, cols * py), F32),
            pltpu.VMEM((cols, py, faces), BF16),
            pltpu.VMEM((chunk, 3 * high, faces), BF16),
            pltpu.VMEM((py, faces), BF16),
            pltpu.VMEM((high, py), F32),
            dma((9,)),
            dma((4, 4)), dma((4, 4)),
            dma((2, cols - 1)), dma((2, cols - 1)),
            dma((9,)), dma((9,)),
            dma((2, WIN)), dma((2, WIN)),
        ],
        compiler_params=pltpu.CompilerParams(
            collective_id=0, has_side_effects=True, vmem_limit_bytes=48 * 1024 * 1024
        ),
        name="slamming",
    )(*operands)
    pressure, plate, motion = pl.pallas_call(
        write,
        out_shape=shapes,
        in_specs=[vmem] * 3,
        out_specs=(hbm,) * 3,
        scratch_shapes=[dma((3,))],
        compiler_params=pltpu.CompilerParams(vmem_limit_bytes=8 * 1024 * 1024),
        name="write_results",
    )(*results)
    return pressure, plate, motion.reshape(faces)


def solution(mesh):
    rows, cols = mesh.shape["row"], mesh.shape["col"]
    placed = (
        P("row", "col", None),
        P("row", "col", None),
        P("row", "col", None),
        P("row", "col"),
        P("row", "col"),
        P("row", "col"),
        P(("row", "col"), None),
        P(("row", "col")),
        P(("row", "col")),
    )
    return jax.shard_map(
        functools.partial(shards, rows, cols),
        mesh=mesh,
        in_specs=placed,
        out_specs=(P("row", "col", None), P("row", "col"), P(("row", "col"))),
        check_vma=False,
    )
```

```python
import functools

import jax
import jax.numpy as jnp
from jax import lax
from jax.experimental import pallas as pl
from jax.experimental.pallas import tpu as pltpu
from jax.sharding import PartitionSpec as P

SWEEPS = 3
PSTEPS = 4
OMEGA = 0.8
BEND = 0.006
LOADC = 0.25

LANES = 128
NEAR = 2
WIN = 2 * NEAR + 1
MESH = pl.DeviceIdType.MESH
NT = (((1,), (1,)), ((), ()))
F32 = jnp.float32
BF16 = jnp.bfloat16


def times(count, body):
    if count <= 32:
        for step in range(count):
            body(step)
    else:
        lax.fori_loop(0, count, lambda step, carry: (body(step), carry)[1], 0)


def three(value):
    a = value.astype(BF16)
    rest = value - a.astype(F32)
    b = rest.astype(BF16)
    c = (rest - b.astype(F32)).astype(BF16)
    return a, b, c


def kernel(
    rows, cols,
    p_hbm, c_hbm, s_hbm, disp_hbm, prev_hbm, thick_hbm, owner_hbm, elem_hbm, wet_hbm,
    out_ref, plate_ref, motion_ref,
    p_ref, c_ref, s_ref, small, faces_in,
    pa, pb, wt, xrecv, ysend, yrecv,
    strip, thin, gbuf, vbuf, ubuf, srecv, lslab, lrecv, win, lwin, onehot, spread, own_hot, uslab,
    lsem, fsend, frecv, gsend, grecv, tsend, trecv, rsend, rrecv, hsend, hrecv,
):
    nx, ny, nz = p_ref.shape
    px, py = small.shape[1:]
    frows = faces_in.shape[1]
    high = cols * px
    last = nx - 1
    reach = SWEEPS
    r, c = lax.axis_index("row"), lax.axis_index("col")

    def row_ok(d):
        return jnp.logical_and(r + d >= 0, r + d < rows)

    def both_ok(dr, dc):
        return jnp.logical_and(row_ok(dr), jnp.logical_and(c + dc >= 0, c + dc < cols))

    shifts = [d for d in range(-NEAR, NEAR + 1) if d != 0]
    corners = [(dr, dc) for dr in (-1, 1) for dc in (-1, 1)]
    blocks = [(-1, 0), (1, 0), (0, -1), (0, 1)] + corners

    loads_in = [
        (c_hbm, c_ref), (p_hbm, p_ref), (s_hbm, s_ref),
        (disp_hbm, small.at[0]), (prev_hbm, small.at[1]), (thick_hbm, small.at[2]),
        (owner_hbm, faces_in.at[0]), (elem_hbm, faces_in.at[1]), (wet_hbm, faces_in.at[2]),
    ]
    loads_in = [pltpu.make_async_copy(a, b, lsem.at[i]) for i, (a, b) in enumerate(loads_in)]
    for copy in loads_in:
        copy.start()

    barrier = pltpu.get_barrier_semaphore()
    peers = cols - 1
    for dr, dc in [(d, 0) for d in shifts] + corners:
        @pl.when(both_ok(dr, dc))
        def _(dr=dr, dc=dc):
            pl.semaphore_signal(barrier, inc=1, device_id=(r + dr, c + dc), device_id_type=MESH)
        peers = peers + both_ok(dr, dc).astype(jnp.int32)

    def greet(step):
        pl.semaphore_signal(barrier, inc=1, device_id=(r, lax.rem(c + 1 + step, cols)), device_id_type=MESH)

    times(cols - 1, greet)

    gives = [r < rows - 1, r > 0, c < cols - 1, c > 0]
    takes = [r > 0, r < rows - 1, c > 0, c < cols - 1]
    fields = [c_ref, p_ref, pa, pb]

    def halo(phase, way):
        if way < 2:
            src = fields[phase].at[last if way == 0 else 0]
            dst = xrecv.at[phase, way]
            to = (r + 1 - 2 * way, c)
        else:
            src = ysend.at[phase, way - 2]
            dst = yrecv.at[phase, way - 2]
            to = (r, c + 1 - 2 * (way - 2))
        return pltpu.make_async_remote_copy(
            src_ref=src, dst_ref=dst, send_sem=fsend.at[phase, way], recv_sem=frecv.at[phase, way],
            device_id=to, device_id_type=MESH,
        )

    def halo_start(phase, ways):
        for way in ways:
            @pl.when(gives[way])
            def _(way=way):
                halo(phase, way).start()

    def halo_wait(phase, ways):
        for way in ways:
            @pl.when(takes[way])
            def _(way=way):
                halo(phase, way).wait_recv()

    def halo_sent(phase):
        for way in range(4):
            @pl.when(gives[way])
            def _(way=way):
                halo(phase, way).wait_send()

    def pack(phase):
        field = fields[phase]
        for x in range(nx):
            ysend[phase, 0, x:x + 1, :] = field[x, ny - 1:ny, :]
            ysend[phase, 1, x:x + 1, :] = field[x, 0:1, :]

    def slot(which, dev):
        return gbuf.at[:, dev] if which == 0 else vbuf.at[dev]

    def gather(which, step):
        return pltpu.make_async_remote_copy(
            src_ref=slot(which, c), dst_ref=slot(which, c), send_sem=gsend.at[which, step],
            recv_sem=grecv.at[which, step], device_id=(r, lax.rem(c + 1 + step, cols)), device_id_type=MESH,
        )

    def gather_start(which):
        times(cols - 1, lambda step: gather(which, step).start())

    def gather_wait(which):
        def one(step):
            frm = lax.rem(c + cols - 1 - step, cols)
            pltpu.make_async_remote_copy(
                src_ref=slot(which, frm), dst_ref=slot(which, frm), send_sem=gsend.at[which, step],
                recv_sem=grecv.at[which, step], device_id=(r, frm), device_id_type=MESH,
            ).wait_recv()
        times(cols - 1, one)

    def gather_sent(which):
        times(cols - 1, lambda step: gather(which, step).wait_send())

    core = lax.rem(c, 2)
    ncol = cols // 2

    def hand(d):
        half = srecv.at[NEAR + d, :, pl.ds(core * ncol, ncol)]
        return pltpu.make_async_remote_copy(
            src_ref=half, dst_ref=half, send_sem=hsend.at[NEAR + d], recv_sem=hrecv.at[NEAR + d],
            device_id=(r, c + 1 - 2 * core), device_id_type=MESH,
        )

    def handed(d):
        half = srecv.at[NEAR + d, :, pl.ds((1 - core) * ncol, ncol)]
        return pltpu.make_async_remote_copy(
            src_ref=half, dst_ref=half, send_sem=hsend.at[NEAR + d], recv_sem=hrecv.at[NEAR + d],
            device_id=(r, c + 1 - 2 * core), device_id_type=MESH,
        )

    def hand_each(act, which):
        for d in shifts:
            @pl.when(row_ok(d))
            def _(d=d):
                act(which(d))

    def along(which, d):
        src = gbuf.at[pl.ds(1, 3), pl.ds(core * ncol, ncol)] if which == 0 else lslab
        dst = srecv.at[NEAR - d, :, pl.ds(core * ncol, ncol)] if which == 0 else lrecv.at[NEAR - d]
        return pltpu.make_async_remote_copy(
            src_ref=src, dst_ref=dst, send_sem=rsend.at[which, NEAR - d], recv_sem=rrecv.at[which, NEAR - d],
            device_id=(r + d, c), device_id_type=MESH,
        )

    def along_each(which, act, back=False):
        for d in shifts:
            @pl.when(row_ok(-d if back else d))
            def _(d=d):
                act(along(which, d))

    far = {-1: (0, reach), 0: (reach, nx), 1: (reach + nx, reach)}

    def skin(dr, dc):
        first = {-1: reach, 0: reach, 1: nx}[dr]
        at, count = far[-dr]
        return pltpu.make_async_remote_copy(
            src_ref=thin.at[1, pl.ds(first, count)], dst_ref=thin.at[1 - dc, pl.ds(at, count)],
            send_sem=tsend.at[3 * dr + dc + 4], recv_sem=trecv.at[3 * dr + dc + 4],
            device_id=(r + dr, c + dc), device_id_type=MESH,
        )

    for way in range(4):
        @pl.when(jnp.logical_not(takes[way]))
        def _(way=way):
            if way < 2:
                for phase in range(4):
                    xrecv[phase, way] = jnp.zeros((ny, nz), F32)
            else:
                for phase in range(4):
                    yrecv[phase, way - 2] = jnp.zeros((nx, nz), F32)
    for dr, dc in blocks:
        @pl.when(jnp.logical_not(both_ok(dr, dc)))
        def _(dr=dr, dc=dc):
            at, count = far[dr]
            thin[1 + dc, at:at + count] = jnp.zeros((count, 8, LANES), F32)
    for d in shifts:
        @pl.when(jnp.logical_not(row_ok(d)))
        def _(d=d):
            srecv[NEAR + d] = jnp.zeros(srecv.shape[1:], F32)
            lrecv[NEAR + d] = jnp.zeros(lrecv.shape[1:], F32)

    for copy in loads_in[:3]:
        copy.wait()
    depth = lax.broadcasted_iota(jnp.int32, (8, LANES), 0)
    along_z = lax.broadcasted_iota(jnp.int32, (ny, nz), 1)
    for x in range(nx):
        layers = jnp.where(
            along_z < 4, p_ref[x], jnp.where(along_z < 8, pltpu.roll(c_ref[x], 4, 1), pltpu.roll(s_ref[x], 8, 1))
        )
        for part, value in enumerate(three(layers)):
            strip[part, x * ny:(x + 1) * ny, :] = value
    pick = jnp.where(
        lax.broadcasted_iota(jnp.int32, (16, nz), 0) == lax.broadcasted_iota(jnp.int32, (16, nz), 1), 1.0, 0.0
    ).astype(BF16)
    moved = [lax.dot_general(pick, strip[part], NT, preferred_element_type=F32) for part in range(3)]
    moved = (moved[0] + moved[1]) + moved[2]
    hull, feed = moved[:8], moved[8:]
    near = lax.broadcasted_iota(jnp.int32, (8, LANES), 1)
    for x in range(nx):
        v = (x // 2) * LANES
        one, two = hull[:, v:v + LANES], feed[:, v:v + LANES]
        if x % 2 == 0:
            two = pltpu.roll(two, ny, 1)
        else:
            one = pltpu.roll(one, ny, 1)
        thin[1, reach + x] = jnp.where(near < ny, one, two)

    pl.semaphore_wait(barrier, peers)

    for dr, dc in blocks:
        @pl.when(both_ok(dr, dc))
        def _(dr=dr, dc=dc):
            skin(dr, dc).start()
    halo_start(0, (0, 1))
    halo_start(1, (0, 1))
    pack(0)
    halo_start(0, (2, 3))
    pack(1)
    halo_start(1, (2, 3))
    for copy in loads_in[3:]:
        copy.wait()
    gbuf[0, c] = (faces_in[0] * (px * py) + faces_in[1]).astype(F32)
    for f in range(3):
        gbuf[1 + f, c] = small[f]
    gather_start(0)

    row_id = lax.broadcasted_iota(jnp.int32, (ny, nz), 0)
    lane_id = lax.broadcasted_iota(jnp.int32, (ny, nz), 1)

    def around(plane, phase, x):
        low = jnp.where(row_id == 0, yrecv[phase, 0, x:x + 1, :], pltpu.roll(plane, 1, 0))
        up = jnp.where(row_id == ny - 1, yrecv[phase, 1, x:x + 1, :], pltpu.roll(plane, ny - 1, 0))
        left = jnp.where(lane_id == 0, 0.0, pltpu.roll(plane, 1, 1))
        right = jnp.where(lane_id == nz - 1, 0.0, pltpu.roll(plane, nz - 1, 1))
        return low, up, left, right

    def beneath(field, phase, x):
        return (
            field[x - 1] if x > 0 else xrecv[phase, 0],
            field[x + 1] if x < last else xrecv[phase, 1],
        )

    def weights(mid, six):
        diag = 3.0 * mid + 0.5 * (((six[0] + six[1]) + (six[2] + six[3])) + (six[4] + six[5]))
        scale = OMEGA / diag
        half = 0.5 * scale
        return scale, [half * (mid + one) for one in six]

    def coefficients(x):
        mid = c_ref[x]
        scale, six = weights(mid, beneath(c_ref, 0, x) + around(mid, 0, x))
        wt[0, x] = scale * s_ref[x]
        for i in range(6):
            wt[1 + i, x] = six[i]

    def sweep(src, dst, phase, x):
        mid = src[x]
        six = beneath(src, phase, x) + around(mid, phase, x)
        total = (1.0 - OMEGA) * mid + wt[0, x]
        for i in range(6):
            total = total + wt[1 + i, x] * six[i]
        dst[x] = total

    halo_wait(0, (2, 3))
    for x in range(1, last):
        coefficients(x)
    halo_wait(1, (2, 3))
    for x in range(1, last):
        sweep(p_ref, pa, 1, x)

    for dr, dc in blocks:
        @pl.when(both_ok(-dr, -dc))
        def _(dr=dr, dc=dc):
            skin(dr, dc).wait_recv()
    half = ny // 2
    ps, cs, ss = [], [], []
    for x in range(nx + 2 * reach):
        left, own, right = thin[0, x], thin[1, x], thin[2, x]
        side = jnp.where(near >= half, left, right)
        middle = jnp.logical_and(near >= half, near < half + ny)
        pc = jnp.where(middle, pltpu.roll(own, half, 1), pltpu.roll(side, half + ny, 1))
        side = jnp.where(near >= ny + half, left, right)
        ss.append(jnp.where(middle, pltpu.roll(own, half + ny, 1), pltpu.roll(side, half, 1)))
        ps.append(jnp.where(depth < 4, pc, 0.0))
        cs.append(jnp.where(depth < 4, pltpu.roll(pc, 4, 0), 0.0))

    def thin_six(field, x):
        mid = field[x]
        return (
            field[x - 1], field[x + 1], pltpu.roll(mid, 1, 1), pltpu.roll(mid, LANES - 1, 1),
            jnp.where(depth == 0, 0.0, pltpu.roll(mid, 1, 0)), pltpu.roll(mid, 7, 0),
        )

    shares = {}
    for x in range(1, nx + 2 * reach - 1):
        scale, six = weights(cs[x], thin_six(cs, x))
        shares[x] = (scale * ss[x], six, cs[x] > 0.0)
    for level in range(1, reach + 1):
        new = list(ps)
        for x in range(level, nx + 2 * reach - level):
            fixed, six, inside = shares[x]
            total = (1.0 - OMEGA) * ps[x] + fixed
            for a, b in zip(six, thin_six(ps, x)):
                total = total + a * b
            new[x] = jnp.where(inside, total, 0.0)
        ps = new
    for j in range(frows):
        even = pltpu.roll(ps[reach + 2 * j], LANES - half, 1)
        odd = pltpu.roll(ps[reach + 2 * j + 1], half, 1)
        face = jnp.where(near < ny, even, odd)[0:1]
        vbuf[c, j:j + 1, :] = face * faces_in[2, j:j + 1, :].astype(F32)
    gather_start(1)

    halo_wait(0, (0, 1))
    for x in (0, last):
        coefficients(x)
    halo_wait(1, (0, 1))
    for x in (0, last):
        sweep(p_ref, pa, 1, x)
    halo_start(2, (0, 1))
    pack(2)
    halo_start(2, (2, 3))

    gather_wait(0)
    along_each(0, lambda copy: copy.start())
    lo_id = lax.broadcasted_iota(jnp.int32, (py, LANES), 0)
    hi_id = lax.broadcasted_iota(jnp.int32, (high, LANES), 0)

    def index(dev, j):
        return gbuf[0, dev, j:j + 1, :].astype(jnp.int32)

    def mark(dev, j):
        return jnp.where(lo_id == lax.rem(index(dev, j), py), 1.0, 0.0).astype(BF16)

    def hot(dev):
        for j in range(frows):
            onehot[dev, :, j * LANES:(j + 1) * LANES] = mark(dev, j)

    times(cols, hot)
    for j in range(frows):
        own_hot[:, j * LANES:(j + 1) * LANES] = mark(c, j)

    gather_wait(1)
    chunk = spread.shape[0]
    loads = jnp.zeros((3 * high, py), F32)
    for base in range(0, cols, chunk):
        def fill(dev):
            for j in range(frows):
                keep = hi_id == lax.div(index(base + dev, j), py)
                for part, v in enumerate(three(vbuf[base + dev, j:j + 1, :])):
                    tile = jnp.where(keep, v.astype(F32), 0.0).astype(BF16)
                    spread[dev, part * high:(part + 1) * high, j * LANES:(j + 1) * LANES] = tile

        times(chunk, fill)
        for dev in range(chunk):
            loads = loads + lax.dot_general(
                spread[dev], onehot[base + dev], NT, preferred_element_type=F32
            )
    slab = loads[:high] + loads[high:2 * high] + loads[2 * high:]
    for dev in range(cols):
        lslab[dev] = slab[dev * px:(dev + 1) * px]
    along_each(1, lambda copy: copy.start())

    along_each(0, lambda copy: copy.wait_recv(), back=True)
    hand_each(lambda copy: copy.start(), hand)

    halo_wait(2, (0, 1, 2, 3))
    for x in (0, last):
        sweep(pa, pb, 2, x)
    halo_start(3, (0, 1))
    for x in range(1, last):
        sweep(pa, pb, 2, x)
    pack(3)
    halo_start(3, (2, 3))

    hand_each(lambda copy: copy.wait_recv(), handed)
    tall, wide = lwin.shape
    win[:, WIN * px:, :] = jnp.zeros((3, tall - WIN * px, wide), F32)
    for w in range(WIN):
        for k in range(cols):
            for f in range(3):
                block = gbuf[1 + f, k] if w == NEAR else srecv[w, f, k]
                win[f, w * px:(w + 1) * px, k * py:(k + 1) * py] = block
    current, previous, thick = win[0], win[1], win[2]
    present = thick > 0.0
    inverse = jnp.where(present, 1.0 / jnp.where(present, thick, 1.0), 0.0)
    stiff = BEND * (thick * thick * thick)
    across = lax.broadcasted_iota(jnp.int32, (tall, wide), 1)

    def laplace(u):
        return (
            pltpu.roll(u, 1, 0) + pltpu.roll(u, tall - 1, 0)
            + jnp.where(across == 0, 0.0, pltpu.roll(u, 1, 1))
            + jnp.where(across == wide - 1, 0.0, pltpu.roll(u, wide - 1, 1)) - 4.0 * u
        )

    def free(now, before):
        return 2.0 * now - before - laplace(stiff * laplace(now)) * inverse

    ahead = free(current, previous)

    halo_wait(3, (2, 3))
    for x in range(1, last):
        sweep(pb, out_ref, 3, x)

    for phase in range(3):
        halo_sent(phase)
    for dr, dc in blocks:
        @pl.when(both_ok(dr, dc))
        def _(dr=dr, dc=dc):
            skin(dr, dc).wait_send()
    for which in range(2):
        gather_sent(which)
    along_each(0, lambda copy: copy.wait_send())
    hand_each(lambda copy: copy.wait_send(), hand)

    along_each(1, lambda copy: copy.wait_recv(), back=True)
    lwin[WIN * px:, :] = jnp.zeros((tall - WIN * px, wide), F32)
    for w in range(WIN):
        for k in range(cols):
            block = lslab[k] if w == NEAR else lrecv[w, k]
            lwin[w * px:(w + 1) * px, k * py:(k + 1) * py] = block
    push = LOADC * lwin[...] * inverse
    previous, current = current, ahead + push
    for _ in range(PSTEPS - 1):
        previous, current = current, free(current, previous) + push
    for dev in range(cols):
        piece = current[NEAR * px:(NEAR + 1) * px, dev * py:(dev + 1) * py]
        ubuf[dev] = piece
        uslab[dev * px:(dev + 1) * px, :] = piece
    plate_ref[...] = ubuf[c]

    parts = three(uslab[...])
    picked = lax.dot_general(
        jnp.concatenate(parts, axis=0), own_hot[...], (((1,), (0,)), ((), ())), preferred_element_type=F32
    )
    picked = picked[:high] + picked[high:2 * high] + picked[2 * high:]
    for j in range(frows):
        keep = hi_id == lax.div(index(c, j), py)
        part = jnp.where(keep, picked[:, j * LANES:(j + 1) * LANES], 0.0)
        motion_ref[j:j + 1, :] = jnp.sum(part, axis=0, keepdims=True)

    halo_wait(3, (0, 1))
    for x in (0, last):
        sweep(pb, out_ref, 3, x)
    halo_sent(3)
    along_each(1, lambda copy: copy.wait_send())


def write(p_ref, plate_ref, motion_ref, p_out, plate_out, motion_out, sem):
    pairs = ((p_ref, p_out), (plate_ref, plate_out), (motion_ref, motion_out))
    copies = [pltpu.make_async_copy(a, b, sem.at[i]) for i, (a, b) in enumerate(pairs)]
    for copy in copies:
        copy.start()
    for copy in copies:
        copy.wait()


def shards(rows, cols, pressure, density, source, disp, prev, thick, owner, elem, wet):
    nx, ny, nz = pressure.shape
    px, py = disp.shape
    faces = elem.shape[0]
    frows = faces // LANES
    assert cols % 2 == 0 and LANES == 2 * ny and nz == LANES and py == LANES
    high = cols * px
    tall = -(-WIN * px // 8) * 8
    chunk = 8 if cols % 8 == 0 else 1
    vmem = pl.BlockSpec(memory_space=pltpu.VMEM)
    hbm = pl.BlockSpec(memory_space=pltpu.HBM)
    dma = pltpu.SemaphoreType.DMA
    shapes = (
        jax.ShapeDtypeStruct(pressure.shape, F32),
        jax.ShapeDtypeStruct(disp.shape, F32),
        jax.ShapeDtypeStruct((frows, LANES), F32),
    )
    tables = [x.reshape(frows, LANES) for x in (owner, elem, wet)]
    operands = [
        pltpu.with_memory_space_constraint(x, pltpu.HBM)
        for x in (pressure, density, source, disp, prev, thick, *tables)
    ]
    results = pl.pallas_call(
        functools.partial(kernel, rows, cols),
        out_shape=tuple(pltpu.VMEM(s.shape, s.dtype) for s in shapes),
        in_specs=[hbm] * 9,
        out_specs=(vmem,) * 3,
        scratch_shapes=[
            pltpu.VMEM((nx, ny, nz), F32),
            pltpu.VMEM((nx, ny, nz), F32),
            pltpu.VMEM((nx, ny, nz), F32),
            pltpu.VMEM((3, px, py), F32),
            pltpu.VMEM((3, frows, LANES), jnp.int32),
            pltpu.VMEM((nx, ny, nz), F32),
            pltpu.VMEM((nx, ny, nz), F32),
            pltpu.VMEM((7, nx, ny, nz), F32),
            pltpu.VMEM((4, 2, ny, nz), F32),
            pltpu.VMEM((4, 2, nx, nz), F32),
            pltpu.VMEM((4, 2, nx, nz), F32),
            pltpu.VMEM((3, nx * ny, nz), BF16),
            pltpu.VMEM((3, nx + 2 * SWEEPS, 8, LANES), F32),
            pltpu.VMEM((4, cols, px, py), F32),
            pltpu.VMEM((cols, frows, LANES), F32),
            pltpu.VMEM((cols, px, py), F32),
            pltpu.VMEM((WIN, 3, cols, px, py), F32),
            pltpu.VMEM((cols, px, py), F32),
            pltpu.VMEM((WIN, cols, px, py), F32),
            pltpu.VMEM((3, tall, cols * py), F32),
            pltpu.VMEM((tall, cols * py), F32),
            pltpu.VMEM((cols, py, faces), BF16),
            pltpu.VMEM((chunk, 3 * high, faces), BF16),
            pltpu.VMEM((py, faces), BF16),
            pltpu.VMEM((high, py), F32),
            dma((9,)),
            dma((4, 4)), dma((4, 4)),
            dma((2, cols - 1)), dma((2, cols - 1)),
            dma((9,)), dma((9,)),
            dma((2, WIN)), dma((2, WIN)),
            dma((WIN,)), dma((WIN,)),
        ],
        compiler_params=pltpu.CompilerParams(
            collective_id=0, has_side_effects=True, vmem_limit_bytes=48 * 1024 * 1024
        ),
        name="slamming",
    )(*operands)
    pressure, plate, motion = pl.pallas_call(
        write,
        out_shape=shapes,
        in_specs=[vmem] * 3,
        out_specs=(hbm,) * 3,
        scratch_shapes=[dma((3,))],
        compiler_params=pltpu.CompilerParams(vmem_limit_bytes=8 * 1024 * 1024),
        name="write_results",
    )(*results)
    return pressure, plate, motion.reshape(faces)


def solution(mesh):
    rows, cols = mesh.shape["row"], mesh.shape["col"]
    placed = (
        P("row", "col", None),
        P("row", "col", None),
        P("row", "col", None),
        P("row", "col"),
        P("row", "col"),
        P("row", "col"),
        P(("row", "col"), None),
        P(("row", "col")),
        P(("row", "col")),
    )
    return jax.shard_map(
        functools.partial(shards, rows, cols),
        mesh=mesh,
        in_specs=placed,
        out_specs=(P("row", "col", None), P("row", "col"), P(("row", "col"))),
        check_vma=False,
    )
```
